512 devices in a mesh: dp: 16 (over x, y), seq: 32 (over z, core).
Axes of the slice: x: 4, y: 4, z: 16, core: 2. Of those that a mesh axis runs over, the one named last changes fastest.
Arguments:
- queries: bfloat16 [16, 4096, 768], P('dp', 'seq'), may hold values from -9 to 9
- keys: bfloat16 [16, 4096, 768], P('dp', 'seq'), may hold values from -9 to 9
- values: bfloat16 [16, 4096, 768], P('dp', 'seq'), may hold values from -6 to 6
- cotangent: bfloat16 [16, 4096, 768], P('dp', 'seq'), may hold values from -6 to 6
- pos_bias: float32 [768], replicated, may hold values from -3 to 3
- owner: int32 [16, 4096], P('dp', 'seq'), may hold values from 0 to 31, as said below
- slot: int32 [16, 4096], P('dp', 'seq'), may hold values from 0 to 127, as said below
- lengths: int32 [16, 4], P('dp'), may hold values from 1 to 2048, 4096 in all within a row
Outputs:
- attended: bfloat16 [16, 4096, 768], P('dp', 'seq')
- grad_queries: bfloat16 [16, 4096, 768], P('dp', 'seq')
- grad_keys: bfloat16 [16, 4096, 768], P('dp', 'seq')
- grad_values: bfloat16 [16, 4096, 768], P('dp', 'seq')
- grad_bias: float32 [768], replicated
The draws below stay inside these ranges and needn't reach their ends.
Inputs may be any that keep to these rules, and one draw needn't show every extreme that they name: Per pack, owner * 128 + slot is a permutation of the pack's positions. The rows of one device (aligned blocks of 128) name any one owner at most 8 times, and in every pack some device names some owner exactly 8 times. `slot`: see owner.
All inputs are finite; a program needn't handle non-finite values.
Results may differ from the reference program's by a relative error of at most 0.017.
The reference program's roundings to bfloat16 on the way count: a program that leaves them out, or rounds other values in their place, can miss the bound.
Values may be sent and summed in bfloat16 or wider, within the bound.
A program may use at most 64 MiB of HBM per device.

```python
import math
import jax
import jax.numpy as jnp
import numpy as np
from jax import lax

HEADS = 12
HEAD_DIM = 64
TOK_DEV = 128
UTTS = 4
HD = 768
PACKS = 16
FRAMES = 4096
WIN = 128


def drawn_rows(key, stamp):
    key = jax.random.fold_in(key, stamp)
    drawn = jax.random.normal(key, (PACKS, FRAMES, HD), jnp.float32)
    return jnp.clip(drawn, -9.0, 9.0)


def draw_queries(key, part):
    return drawn_rows(key, 11).astype(jnp.bfloat16)


def draw_keys(key, part):
    return drawn_rows(key, 12).astype(jnp.bfloat16)


def routing_tables(key):
    peers = FRAMES // TOK_DEV
    base = TOK_DEV // peers

    def one_pack(pkey):
        first, second, third = jax.random.split(pkey, 3)
        half = jnp.ones((peers // 2,), jnp.int32)
        signs = jax.random.permutation(first, jnp.concatenate([half, -half]))
        source = jnp.arange(peers, dtype=jnp.int32)[:, None]
        target = jnp.arange(peers, dtype=jnp.int32)[None, :]
        counts = base + base * signs[(target - source) % peers]
        inclusive = jnp.cumsum(counts, 1)
        exclusive = inclusive - counts
        arrive = jnp.cumsum(counts, 0) - counts
        index = jnp.arange(TOK_DEV, dtype=jnp.int32)
        dest = jnp.sum((index[None, :, None] >= inclusive[:, None, :]).astype(jnp.int32), 2)
        rank = index[None, :] - jnp.take_along_axis(exclusive, dest, 1)
        landing = jnp.take_along_axis(arrive, dest, 1) + rank
        slot_perm = jax.vmap(lambda k: jax.random.permutation(k, TOK_DEV))(jax.random.split(second, peers))
        slot_value = slot_perm[dest, landing]
        row_perm = jax.vmap(lambda k: jax.random.permutation(k, TOK_DEV))(jax.random.split(third, peers))
        lines = jnp.arange(peers, dtype=jnp.int32)[:, None]
        owners = jnp.zeros((peers, TOK_DEV), jnp.int32).at[lines, row_perm].set(dest)
        slots = jnp.zeros((peers, TOK_DEV), jnp.int32).at[lines, row_perm].set(slot_value)
        return (owners.reshape(FRAMES), slots.reshape(FRAMES))
    return jax.vmap(one_pack)(jax.random.split(jax.random.fold_in(key, 5), PACKS))


def draw_owner(key, part):
    return routing_tables(key)[0]


def draw_slot(key, part):
    return routing_tables(key)[1]


def steps_of(own_key, extent, pieces, low, high):
    level, own = 1.0, jax.random.fold_in(own_key, 6)
    for axis_at, blocks in pieces:
        steps = jnp.exp(jax.random.uniform(jax.random.fold_in(own, axis_at), (blocks,), jnp.float32, low / len(pieces), high / len(pieces)))
        level = level * jnp.repeat(steps, extent[axis_at] // blocks).reshape([-1 if axis == axis_at else 1 for axis in range(len(extent))])
    return level


def length_profile(number_of, total, bound, lean):
    weights = [(1 << 20) // math.isqrt(standing ** lean) + 1 for standing in range(2, number_of + 1)]
    surplus, holding = total - bound - (number_of - 1), [1] * (number_of - 1)
    while surplus > 0:
        free = [i for i in range(number_of - 1) if holding[i] < bound]
        pool, left = sum([weights[i] for i in free]), surplus
        for i in free:
            more = min(bound - holding[i], max(1, left * weights[i] // pool), surplus)
            holding[i] = holding[i] + more
            surplus = surplus - more
    return np.array([bound] + holding)


def uneven_parts(rng, count, total, bound, slope):
    if count == 2:
        one = jax.random.randint(rng, (), max(1, total - bound), min(bound, total - 1) + 1)
        return jnp.stack([one, total - one])
    tallies = jnp.asarray(length_profile(count, total, bound, slope), jnp.int32)
    couples = (count - 1) // 2
    giver, sink = tallies[1:1 + 2 * couples:2], tallies[2:2 + 2 * couples:2]
    room = jnp.minimum(giver - 1, bound - sink)
    shifted = jax.random.randint(jax.random.fold_in(rng, 1), (couples,), 0, 1 << 20) % (room + 1)
    tallies = tallies.at[1:1 + 2 * couples:2].set(giver - shifted).at[2:2 + 2 * couples:2].set(sink + shifted)
    return tallies[jax.random.permutation(jax.random.fold_in(rng, 2), count)]


def gaussian(rng, shape, width, most, pieces=(), held_as=jnp.bfloat16):
    entries = width * jax.random.normal(rng, shape, jnp.float32)
    if pieces:
        entries = entries * steps_of(rng, shape, pieces, -0.22, 0.18)
    return jnp.clip(entries, -most, most).astype(held_as)


def setup_inputs(seed: int = 0) -> dict:
    key_list = jax.random.split(jax.random.key(seed), 9)
    queries = draw_queries(jax.random.fold_in(key_list[8], 71), 0)
    keys = draw_keys(jax.random.fold_in(key_list[8], 71), 0)
    values = gaussian(key_list[2], (PACKS, FRAMES, HD), 1.0, 6.0, ((0, 16), (1, 32)))
    cotangent = gaussian(key_list[3], (PACKS, FRAMES, HD), 1.0, 6.0, ((0, 16), (1, 32)))
    pos_bias = gaussian(key_list[4], (HD,), 0.5, 3.0, (), jnp.float32)
    owner = draw_owner(jax.random.fold_in(key_list[8], 71), 0)
    slot = draw_slot(jax.random.fold_in(key_list[8], 71), 0)
    lengths = jax.vmap(lambda own: uneven_parts(own, UTTS, FRAMES, FRAMES // 2, 2))(jax.random.split(key_list[7], PACKS)).reshape((PACKS, UTTS)).astype(jnp.int32)
    return {"queries": queries, "keys": keys, "values": values, "cotangent": cotangent, "pos_bias": pos_bias, "owner": owner, "slot": slot, "lengths": lengths}


def head_forward(qh, kh, vh, mask):
    scale = 1.0 / jnp.sqrt(jnp.float32(qh.shape[-1]))
    s = lax.dot_general(qh, kh, (((1,), (1,)), ((), ())), preferred_element_type=jnp.float32) * scale
    s = jnp.where(mask, s, -1e+30)
    top = lax.optimization_barrier(jnp.max(s, axis=1))
    lse = top + jnp.log(lax.optimization_barrier(jnp.sum(jnp.exp(s - top[:, None]), axis=1)))
    p = jnp.where(mask, jnp.exp(s - lse[:, None]), 0.0)
    o = jnp.dot(p.astype(jnp.bfloat16), vh, preferred_element_type=jnp.float32).astype(jnp.bfloat16)
    return (o, lse)

def head_backward(qh, kh, vh, doh, oh, lse, mask):
    scale = 1.0 / jnp.sqrt(jnp.float32(qh.shape[-1]))
    s = lax.dot_general(qh, kh, (((1,), (1,)), ((), ())), preferred_element_type=jnp.float32) * scale
    p = jnp.where(mask, jnp.exp(s - lse[:, None]), 0.0)
    prob = p.astype(jnp.bfloat16)
    dpm = lax.dot_general(doh, vh, (((1,), (1,)), ((), ())), preferred_element_type=jnp.float32)
    delta = lax.optimization_barrier(jnp.sum(doh.astype(jnp.float32) * oh.astype(jnp.float32), axis=1))
    ds = (p * (dpm - delta[:, None]) * scale).astype(jnp.bfloat16)
    dq = jnp.dot(ds, kh, preferred_element_type=jnp.float32)
    dkw = lax.dot_general(ds, qh, (((0,), (0,)), ((), ())), preferred_element_type=jnp.float32)
    dvw = lax.dot_general(prob, doh, (((0,), (0,)), ((), ())), preferred_element_type=jnp.float32)
    return (dq, dkw, dvw)

def heads_first(x):
    return x.reshape(x.shape[0], HEADS, HEAD_DIM).transpose(1, 0, 2)

def heads_last(x):
    return x.transpose(1, 0, 2).reshape(x.shape[1], HEADS * HEAD_DIM)

def one_pack(q, k, v, g, own, sl, ln, pos_bias):
    rows = TOK_DEV
    position = (own * rows + sl).astype(jnp.int32)
    zero = jnp.zeros((FRAMES, HD), jnp.bfloat16)
    qa = zero.at[position].set(q)
    ka = zero.at[position].set(k)
    va = zero.at[position].set(v)
    ga = zero.at[position].set(g)
    biased = (qa.astype(jnp.float32) + pos_bias[None, :]).astype(jnp.bfloat16)
    ends = jnp.cumsum(ln)
    pad = jnp.zeros((rows, HD), jnp.bfloat16)
    kp = jnp.concatenate([pad, ka, pad], 0)
    vp = jnp.concatenate([pad, va, pad], 0)

    def block(b):
        start = (b * rows).astype(jnp.int32)
        qb = lax.dynamic_slice_in_dim(biased, start, rows, 0)
        gb = lax.dynamic_slice_in_dim(ga, start, rows, 0)
        kw = lax.dynamic_slice_in_dim(kp, start, 3 * rows, 0)
        vw = lax.dynamic_slice_in_dim(vp, start, 3 * rows, 0)
        own_pos = start + jnp.arange(rows, dtype=jnp.int32)
        win_pos = start - rows + jnp.arange(3 * rows, dtype=jnp.int32)
        seg_q = lax.optimization_barrier(jnp.sum((own_pos[:, None] >= ends[None, :]).astype(jnp.int32), 1))
        seg_k = lax.optimization_barrier(jnp.sum((win_pos[:, None] >= ends[None, :]).astype(jnp.int32), 1))
        valid = (win_pos >= 0) & (win_pos < FRAMES)
        mask = (jnp.abs(own_pos[:, None] - win_pos[None, :]) <= WIN) & (seg_q[:, None] == seg_k[None, :]) & valid[None, :]
        qh, kh, vh, gh = (heads_first(qb), heads_first(kw), heads_first(vw), heads_first(gb))
        oh, lse = lax.map(lambda a: head_forward(a[0], a[1], a[2], mask), (qh, kh, vh))
        dq, dkw, dvw = lax.map(lambda a: head_backward(a[0], a[1], a[2], a[3], a[4], a[5], mask), (qh, kh, vh, gh, oh, lse))
        return (heads_last(oh), heads_last(dq), heads_last(dkw), heads_last(dvw))
    nblk = FRAMES // rows
    o, dq, dkw, dvw = lax.map(block, jnp.arange(nblk, dtype=jnp.int32))

    def combine(w):
        zeros = jnp.zeros((1, rows, HD), jnp.float32)
        prev = jnp.concatenate([zeros, w[:-1, 2 * rows:]], 0)
        nxt = jnp.concatenate([w[1:, :rows], zeros], 0)
        return (w[:, rows:2 * rows] + prev + nxt).reshape(FRAMES, HD)
    dk = combine(dkw)
    dv = combine(dvw)
    o = o.reshape(FRAMES, HD)
    dq = dq.reshape(FRAMES, HD)
    return (o[position], dq[position].astype(jnp.bfloat16), dk[position].astype(jnp.bfloat16), dv[position].astype(jnp.bfloat16), lax.optimization_barrier(jnp.sum(dq, 0)))

def reference(queries, keys, values, cotangent, pos_bias, owner, slot, lengths):

    def run(a):
        return one_pack(a[0], a[1], a[2], a[3], a[4], a[5], a[6], pos_bias)
    o, dq, dk, dv, bias_part = lax.map(run, (queries, keys, values, cotangent, owner, slot, lengths))
    return (o, dq, dk, dv, lax.optimization_barrier(jnp.sum(bias_part, 0)))
```

```python
import jax
import jax.numpy as jnp
from jax import lax
from jax.experimental import pallas as pl
from jax.experimental.pallas import tpu as pltpu
from jax.sharding import PartitionSpec as P

HEAD_DIM = 64
ROWS = 128
WIDTH = 768
LANES = 128
CHUNKS = WIDTH // LANES
PEERS = 32
PACKS = 16
ROOM = 8
PAIRS = PEERS * 2 * ROOM
AHEAD = 3
MESH = pl.DeviceIdType.MESH
BF16 = jnp.bfloat16
F32 = jnp.float32


def dot(a, b):
    return jnp.dot(a, b, preferred_element_type=F32)


def dot_t(a, b):
    return lax.dot_general(a, b, (((1,), (1,)), ((), ())), preferred_element_type=F32)


def t_dot(a, b):
    return lax.dot_general(a, b, (((0,), (0,)), ((), ())), preferred_element_type=F32)


def iota(shape, dim):
    return lax.broadcasted_iota(jnp.int32, shape, dim)


def kernel(
    q_ref, k_ref, v_ref, g_ref, bias_ref, owner_ref, slot_ref, lengths_ref,
    o_out, dq_out, dk_out, dv_out, gb_out,
    pack, unpack, land, unland, live,
    marks_out, marks_in,
    sent, got, back_sent, back_got,
    kv, part_sent, part_got, own_parts, o_keep, dq_keep,
    gb, gb_seq, gb_pack, gb_dp,
    marks_ss, marks_rs, sent_s, got_s, back_ss, back_rs,
    kv_ss, kv_rs, part_ss, part_rs, seq_ss, seq_rs, dp_ss, dp_rs,
):
    dp = lax.axis_index("dp")
    me = lax.axis_index("seq")
    left = lax.rem(me + PEERS - 1, PEERS)
    right = lax.rem(me + 1, PEERS)

    barrier = pltpu.get_barrier_semaphore()

    def greet_seq(o, _):
        peer = lax.rem(me + o, PEERS)
        pl.semaphore_signal(barrier, inc=1, device_id=(dp, peer), device_id_type=MESH)
        return 0

    def greet_dp(o, _):
        peer = lax.rem(dp + o, PACKS)
        pl.semaphore_signal(barrier, inc=1, device_id=(peer, me), device_id_type=MESH)
        return 0

    lax.fori_loop(1, PEERS, greet_seq, 0)
    lax.fori_loop(1, PACKS, greet_dp, 0)

    owner = owner_ref[...]
    slot = slot_ref[...]
    to = (jnp.broadcast_to(owner, (PEERS, ROWS)) == iota((PEERS, ROWS), 0)).astype(F32)
    before = (iota((ROWS, ROWS), 0) < iota((ROWS, ROWS), 1)).astype(BF16)
    earlier = dot(to.astype(BF16), before)
    rank = jnp.sum(to * earlier, axis=0, keepdims=True).astype(jnp.int32)
    place = owner * (2 * ROOM) + rank
    places = jnp.concatenate([place, place + ROOM], axis=1)
    chosen = (jnp.broadcast_to(places, (PAIRS, 2 * ROWS)) == iota((PAIRS, 2 * ROWS), 0)).astype(F32)
    pack[...] = chosen.astype(BF16)
    unpack[...] = jnp.transpose(chosen).astype(BF16)
    ranked = jnp.where(
        jnp.broadcast_to(rank, (ROWS, ROWS)) == iota((ROWS, ROWS), 0),
        jnp.broadcast_to(slot + 1, (ROWS, ROWS)),
        0,
    ).astype(F32)
    marks = dot_t(to.astype(BF16), ranked.astype(BF16))
    for peer in range(PEERS):
        marks_out[peer] = marks[peer : peer + 1]
    marks_in[me] = marks_out[me]

    first = me * ROWS
    row_pos = first + iota((ROWS, 3 * ROWS), 0)
    col_pos = first - ROWS + iota((ROWS, 3 * ROWS), 1)
    row_seg = jnp.zeros((ROWS, 3 * ROWS), jnp.int32)
    col_seg = jnp.zeros((ROWS, 3 * ROWS), jnp.int32)
    end = jnp.int32(0)
    for utt in range(4):
        end = end + lengths_ref[0, utt]
        row_seg = row_seg + (row_pos >= end).astype(jnp.int32)
        col_seg = col_seg + (col_pos >= end).astype(jnp.int32)
    alive = (
        (jnp.abs(row_pos - col_pos) <= ROWS)
        & (row_seg == col_seg)
        & (col_pos >= 0)
        & (col_pos < PEERS * ROWS)
    )
    masked = jnp.where(alive, 0.0, -1e30).astype(F32)
    live[0:ROWS] = masked
    live[ROWS:] = masked
    gb[...] = jnp.zeros_like(gb)

    def lanes(c):
        return pl.ds(pl.multiple_of(c * LANES, LANES), LANES)

    def fill(c):
        x = jnp.concatenate(
            [
                jnp.concatenate([q_ref[:, lanes(c)], v_ref[:, lanes(c)]], axis=1),
                jnp.concatenate([k_ref[:, lanes(c)], g_ref[:, lanes(c)]], axis=1),
            ],
            axis=0,
        )
        packed = dot(pack[...], x).astype(BF16)
        sent[c] = packed.reshape(PEERS, 2 * ROOM, 2 * LANES)
        got[c, me] = sent[c, me]

    def send(c):
        def to_peer(o, _):
            peer = lax.rem(me + o, PEERS)
            pltpu.make_async_remote_copy(
                src_ref=sent.at[c, peer], dst_ref=got.at[c, me],
                send_sem=sent_s.at[c], recv_sem=got_s.at[c],
                device_id=(dp, peer), device_id_type=MESH,
            ).start()
            return 0

        lax.fori_loop(1, PEERS, to_peer, 0)

    def many(src, dst, send_sem, recv_sem, count):
        return pltpu.make_async_remote_copy(
            src_ref=src.at[pl.ds(0, count)], dst_ref=dst.at[pl.ds(0, count)],
            send_sem=send_sem, recv_sem=recv_sem,
            device_id=(dp, right), device_id_type=MESH,
        )

    def kv_copy(c, to_right):
        return pltpu.make_async_remote_copy(
            src_ref=kv.at[c, 1], dst_ref=kv.at[c, 0 if to_right else 2],
            send_sem=kv_ss.at[c, int(to_right)], recv_sem=kv_rs.at[c, int(to_right)],
            device_id=(dp, right if to_right else left), device_id_type=MESH,
        )

    def part_copy(c, to_right):
        side = int(to_right)
        return pltpu.make_async_remote_copy(
            src_ref=part_sent.at[c, side], dst_ref=part_got.at[c, side],
            send_sem=part_ss.at[c, side], recv_sem=part_rs.at[c, side],
            device_id=(dp, right if to_right else left), device_id_type=MESH,
        )

    fill(0)
    pl.semaphore_wait(barrier, PEERS - 1 + PACKS - 1)

    def send_marks(o, _):
        peer = lax.rem(me + o, PEERS)
        pltpu.make_async_remote_copy(
            src_ref=marks_out.at[peer], dst_ref=marks_in.at[me],
            send_sem=marks_ss, recv_sem=marks_rs,
            device_id=(dp, peer), device_id_type=MESH,
        ).start()
        return 0

    lax.fori_loop(1, PEERS, send_marks, 0)
    send(0)

    def early(c, _):
        fill(c)
        send(c)
        return 0

    lax.fori_loop(1, AHEAD, early, 0)

    many(marks_out, marks_in, marks_ss, marks_rs, PEERS - 1).wait_recv()
    arrived = jnp.concatenate([marks_in[peer] for peer in range(PEERS)], axis=0)
    spread = (iota((PAIRS, PEERS), 0) // (2 * ROOM) == iota((PAIRS, PEERS), 1)).astype(BF16)
    wide = dot(spread, arrived.astype(BF16))
    wide = jnp.where(iota((PAIRS, ROWS), 0) % ROOM == iota((PAIRS, ROWS), 1), wide, 0.0)
    mark = jnp.sum(wide, axis=1, keepdims=True).astype(jnp.int32)
    second = iota((PAIRS, 1), 0) % (2 * ROOM) // ROOM
    landing = jnp.where(mark > 0, mark - 1 + ROWS * second, -1)
    lands = (jnp.broadcast_to(landing, (PAIRS, 2 * ROWS)) == iota((PAIRS, 2 * ROWS), 1)).astype(F32)
    unland[...] = lands.astype(BF16)
    land[...] = jnp.transpose(lands).astype(BF16)

    low = iota((ROWS, LANES), 1) < HEAD_DIM

    def stacked(x):
        zero = jnp.zeros_like(x)
        return jnp.concatenate([jnp.where(low, x, zero), jnp.where(low, zero, x)], axis=0)

    def merged(x):
        return jnp.where(low, x[:ROWS], x[ROWS:])

    def arrive(c):
        many(sent.at[c], got.at[c], sent_s.at[c], got_s.at[c], PEERS - 1).wait_recv()
        x = dot(land[...], got[c].reshape(PAIRS, 2 * LANES))
        biased = (x[:ROWS, :LANES] + bias_ref[:, lanes(c)]).astype(BF16)
        o_keep[c] = biased
        dq_keep[c] = x[ROWS:, LANES:].astype(BF16)
        kv[c, 1, 0:ROWS] = x[ROWS:, :LANES].astype(BF16)
        kv[c, 1, ROWS:] = x[:ROWS, LANES:].astype(BF16)
        kv_copy(c, True).start()
        kv_copy(c, False).start()

    def attend(c):
        kv_copy(c, True).wait_recv()
        kv_copy(c, False).wait_recv()
        keys = jnp.concatenate([kv[c, side, 0:ROWS] for side in range(3)], axis=0)
        values = jnp.concatenate([kv[c, side, ROWS:] for side in range(3)], axis=0)
        b = stacked(o_keep[c].astype(F32)).astype(BF16)
        g32 = stacked(dq_keep[c].astype(F32))
        g = g32.astype(BF16)
        scale = 1.0 / HEAD_DIM**0.5
        s = dot_t(b, keys) * scale + live[...]
        top = jnp.max(s, axis=1, keepdims=True)
        e = jnp.exp(s - top)
        p = e * (1.0 / jnp.sum(e, axis=1, keepdims=True))
        prob = p.astype(BF16)
        o = merged(dot(prob, values)).astype(BF16)
        o32 = o.astype(F32)
        delta = jnp.sum(g32 * jnp.concatenate([o32, o32], axis=0), axis=1, keepdims=True)
        ds = (p * (dot_t(g, values) - delta) * scale).astype(BF16)
        dq = merged(dot(ds, keys))
        dk = t_dot(ds, b)
        dv = t_dot(prob, g)
        for side, at in ((0, 0), (1, 2 * ROWS)):
            part_sent[c, side, 0:ROWS] = dk[at : at + ROWS].astype(BF16)
            part_sent[c, side, ROWS:] = dv[at : at + ROWS].astype(BF16)
        part_copy(c, True).start()
        part_copy(c, False).start()
        own_parts[c, 0:ROWS] = dk[ROWS : 2 * ROWS]
        own_parts[c, ROWS:] = dv[ROWS : 2 * ROWS]
        o_keep[c] = o
        dq_keep[c] = dq.astype(BF16)
        gb[pl.ds(c, 1), :] = jnp.sum(dq, axis=0, keepdims=True)

    def give_back(c):
        part_copy(c, True).wait_recv()
        part_copy(c, False).wait_recv()
        total = own_parts[c] + part_got[c, 0].astype(F32) + part_got[c, 1].astype(F32)
        total = total.astype(BF16)
        x = jnp.concatenate(
            [
                jnp.concatenate([o_keep[c], total[:ROWS]], axis=1),
                jnp.concatenate([dq_keep[c], total[ROWS:]], axis=1),
            ],
            axis=0,
        )
        back_sent[c] = dot(unland[...], x).astype(BF16).reshape(PEERS, 2 * ROOM, 2 * LANES)
        back_got[c, me] = back_sent[c, me]

        def to_peer(o, _):
            peer = lax.rem(me + o, PEERS)
            pltpu.make_async_remote_copy(
                src_ref=back_sent.at[c, peer], dst_ref=back_got.at[c, me],
                send_sem=back_ss.at[c], recv_sem=back_rs.at[c],
                device_id=(dp, peer), device_id_type=MESH,
            ).start()
            return 0

        lax.fori_loop(1, PEERS, to_peer, 0)

    def finish(c):
        many(back_sent.at[c], back_got.at[c], back_ss.at[c], back_rs.at[c], PEERS - 1).wait_recv()
        x = dot(unpack[...], back_got[c].reshape(PAIRS, 2 * LANES)).astype(BF16)
        o_out[:, lanes(c)] = x[:ROWS, :LANES]
        dk_out[:, lanes(c)] = x[:ROWS, LANES:]
        dq_out[:, lanes(c)] = x[ROWS:, :LANES]
        dv_out[:, lanes(c)] = x[ROWS:, LANES:]

    def step(i, _):
        @pl.when(i + AHEAD < CHUNKS)
        def _():
            fill(i + AHEAD)
            send(i + AHEAD)

        @pl.when(i < CHUNKS)
        def _():
            arrive(i)

        @pl.when((i >= 1) & (i < CHUNKS + 1))
        def _():
            attend(i - 1)

        @pl.when(i >= 2)
        def _():
            give_back(i - 2)

        return 0

    lax.fori_loop(0, CHUNKS + 2, step, 0)

    gb_seq[me] = gb[...]

    def share_seq(o, _):
        peer = lax.rem(me + o, PEERS)
        pltpu.make_async_remote_copy(
            src_ref=gb, dst_ref=gb_seq.at[me],
            send_sem=seq_ss, recv_sem=seq_rs,
            device_id=(dp, peer), device_id_type=MESH,
        ).start()
        return 0

    lax.fori_loop(1, PEERS, share_seq, 0)

    def finish_one(c, _):
        finish(c)
        return 0

    lax.fori_loop(0, CHUNKS - 1, finish_one, 0)

    many(gb_seq, gb_seq, seq_ss, seq_rs, PEERS - 1).wait_recv()
    gb_pack[...] = jnp.sum(gb_seq[...], axis=0)
    gb_dp[dp] = gb_pack[...]

    def share_dp(o, _):
        peer = lax.rem(dp + o, PACKS)
        pltpu.make_async_remote_copy(
            src_ref=gb_pack, dst_ref=gb_dp.at[dp],
            send_sem=dp_ss, recv_sem=dp_rs,
            device_id=(peer, me), device_id_type=MESH,
        ).start()
        return 0

    lax.fori_loop(1, PACKS, share_dp, 0)
    finish(CHUNKS - 1)
    many(gb_dp, gb_dp, dp_ss, dp_rs, PACKS - 1).wait_recv()
    gb_out[...] = jnp.sum(gb_dp[...], axis=0)

    many(marks_out, marks_in, marks_ss, marks_rs, PEERS - 1).wait_send()
    many(gb_seq, gb_seq, seq_ss, seq_rs, PEERS - 1).wait_send()
    many(gb_dp, gb_dp, dp_ss, dp_rs, PACKS - 1).wait_send()

    def left_all(c, _):
        many(sent.at[c], got.at[c], sent_s.at[c], got_s.at[c], PEERS - 1).wait_send()
        many(back_sent.at[c], back_got.at[c], back_ss.at[c], back_rs.at[c], PEERS - 1).wait_send()
        for to_right in (True, False):
            kv_copy(c, to_right).wait_send()
            part_copy(c, to_right).wait_send()
        return 0

    lax.fori_loop(0, CHUNKS, left_all, 0)


def body(queries, keys, values, cotangent, pos_bias, owner, slot, lengths):
    vmem = pl.BlockSpec(memory_space=pltpu.VMEM)
    smem = pl.BlockSpec(memory_space=pltpu.SMEM)
    rows = jax.ShapeDtypeStruct((ROWS, WIDTH), BF16)
    dma = pltpu.SemaphoreType.DMA
    block = (CHUNKS, PEERS, 2 * ROOM, 2 * LANES)
    o, dq, dk, dv, gb = pl.pallas_call(
        kernel,
        out_shape=(rows, rows, rows, rows, jax.ShapeDtypeStruct((8, LANES), F32)),
        in_specs=[vmem] * 7 + [smem],
        out_specs=(vmem,) * 5,
        scratch_shapes=[
            pltpu.VMEM((PAIRS, 2 * ROWS), BF16),
            pltpu.VMEM((2 * ROWS, PAIRS), BF16),
            pltpu.VMEM((2 * ROWS, PAIRS), BF16),
            pltpu.VMEM((PAIRS, 2 * ROWS), BF16),
            pltpu.VMEM((2 * ROWS, 3 * ROWS), F32),
            pltpu.VMEM((PEERS, 1, LANES), F32),
            pltpu.VMEM((PEERS, 1, LANES), F32),
            pltpu.VMEM(block, BF16),
            pltpu.VMEM(block, BF16),
            pltpu.VMEM(block, BF16),
            pltpu.VMEM(block, BF16),
            pltpu.VMEM((CHUNKS, 3, 2 * ROWS, LANES), BF16),
            pltpu.VMEM((CHUNKS, 2, 2 * ROWS, LANES), BF16),
            pltpu.VMEM((CHUNKS, 2, 2 * ROWS, LANES), BF16),
            pltpu.VMEM((CHUNKS, 2 * ROWS, LANES), F32),
            pltpu.VMEM((CHUNKS, ROWS, LANES), BF16),
            pltpu.VMEM((CHUNKS, ROWS, LANES), BF16),
            pltpu.VMEM((8, LANES), F32),
            pltpu.VMEM((PEERS, 8, LANES), F32),
            pltpu.VMEM((8, LANES), F32),
            pltpu.VMEM((PACKS, 8, LANES), F32),
            dma, dma,
            dma((CHUNKS,)), dma((CHUNKS,)), dma((CHUNKS,)), dma((CHUNKS,)),
            dma((CHUNKS, 2)), dma((CHUNKS, 2)), dma((CHUNKS, 2)), dma((CHUNKS, 2)),
            dma, dma, dma, dma,
        ],
        compiler_params=pltpu.CompilerParams(
            collective_id=0, has_side_effects=True, vmem_limit_bytes=40 << 20
        ),
    )(
        queries[0], keys[0], values[0], cotangent[0],
        pos_bias[None, :], owner, slot, lengths,
    )
    return o[None], dq[None], dk[None], dv[None], gb[:CHUNKS].reshape(WIDTH)


def solution(mesh):
    rows = P("dp", "seq", None)
    in_specs = (rows, rows, rows, rows, P(), P("dp", "seq"), P("dp", "seq"), P("dp", None))
    out_specs = (rows, rows, rows, rows, P())
    return jax.shard_map(body, mesh=mesh, in_specs=in_specs, out_specs=out_specs, check_vma=False)
```

```python
import jax
import jax.numpy as jnp
from jax import lax
from jax.experimental import pallas as pl
from jax.experimental.pallas import tpu as pltpu
from jax.sharding import PartitionSpec as P

HEAD_DIM = 64
ROWS = 128
WIDTH = 768
LANES = 128
WIDE = 256
CHUNKS = WIDTH // WIDE
PEERS = 32
PACKS = 16
ROOM = 8
PAIRS = PEERS * 2 * ROOM
MESH = pl.DeviceIdType.MESH
BF16 = jnp.bfloat16
F32 = jnp.float32


def dot(a, b):
    return jnp.dot(a, b, preferred_element_type=F32)


def dot_t(a, b):
    return lax.dot_general(a, b, (((1,), (1,)), ((), ())), preferred_element_type=F32)


def t_dot(a, b):
    return lax.dot_general(a, b, (((0,), (0,)), ((), ())), preferred_element_type=F32)


def iota(shape, dim):
    return lax.broadcasted_iota(jnp.int32, shape, dim)


def kernel(
    q_hbm, k_hbm, v_hbm, g_hbm, bias_hbm, owner_hbm, slot_hbm, lengths_hbm,
    o_hbm, dq_hbm, dk_hbm, dv_hbm, gb_out,
    x, y, pack, unpack, land, unland, live,
    marks_out, marks_in,
    sent, got, back_sent, back_got,
    kv, part_sent, part_got, own_parts, result,
    gb, gb_dp, gb_packs, gb_seq,
    bias_flat, bias, owner_ref, slot_ref, lengths_ref,
    small_s, in_s, out_s,
    marks_ss, marks_rs, sent_s, got_s, back_ss, back_rs,
    kv_ss, kv_rs, part_ss, part_rs, seq_ss, seq_rs, dp_ss, dp_rs,
):
    dp = lax.axis_index("dp")
    me = lax.axis_index("seq")
    left = lax.rem(me + PEERS - 1, PEERS)
    right = lax.rem(me + 1, PEERS)

    barrier = pltpu.get_barrier_semaphore()

    def greet_seq(o, _):
        peer = lax.rem(me + o, PEERS)
        pl.semaphore_signal(barrier, inc=1, device_id=(dp, peer), device_id_type=MESH)
        return 0

    def greet_dp(o, _):
        peer = lax.rem(dp + o, PACKS)
        pl.semaphore_signal(barrier, inc=1, device_id=(peer, me), device_id_type=MESH)
        return 0

    lax.fori_loop(1, PEERS, greet_seq, 0)
    lax.fori_loop(1, PACKS, greet_dp, 0)

    def wide(c):
        return pl.ds(pl.multiple_of(c * WIDE, WIDE), WIDE)

    small = [
        pltpu.make_async_copy(src, dst, small_s.at[i])
        for i, (src, dst) in enumerate(
            [
                (owner_hbm, owner_ref),
                (slot_hbm, slot_ref),
                (bias_hbm, bias_flat),
                (lengths_hbm, lengths_ref),
            ]
        )
    ]
    for copy in small:
        copy.start()

    inputs = (k_hbm, v_hbm, q_hbm, g_hbm)

    def load(array, c):
        return pltpu.make_async_copy(
            inputs[array].at[:, wide(c)],
            x.at[array // 2, c, pl.ds(array % 2 * ROWS, ROWS)],
            in_s.at[array, c],
        )

    for half in range(2):
        for c in range(CHUNKS):
            load(2 * half, c).start()
            load(2 * half + 1, c).start()

    for copy in small:
        copy.wait()
    owner = owner_ref[...]
    slot = slot_ref[...]
    to = (jnp.broadcast_to(owner, (PEERS, ROWS)) == iota((PEERS, ROWS), 0)).astype(F32)
    before = (iota((ROWS, ROWS), 0) < iota((ROWS, ROWS), 1)).astype(BF16)
    earlier = dot(to.astype(BF16), before)
    rank = jnp.sum(to * earlier, axis=0, keepdims=True).astype(jnp.int32)
    place = owner * (2 * ROOM) + rank
    places = jnp.concatenate([place, place + ROOM], axis=1)
    chosen = (jnp.broadcast_to(places, (PAIRS, 2 * ROWS)) == iota((PAIRS, 2 * ROWS), 0)).astype(F32)
    pack[...] = chosen.astype(BF16)

    def fill(half, c):
        load(2 * half, c).wait()
        load(2 * half + 1, c).wait()
        packed = dot(pack[...], x[half, c]).astype(BF16)
        sent[half, c] = packed.reshape(PEERS, 2 * ROOM, WIDE)
        got[half, c, me] = sent[half, c, me]

    def scatter(src, dst, send_sem, recv_sem):
        def to_peer(o, _):
            peer = lax.rem(me + 16 + (o // 2) * (1 - 2 * lax.rem(o, 2)) + PEERS, PEERS)
            pltpu.make_async_remote_copy(
                src_ref=src.at[peer], dst_ref=dst.at[me],
                send_sem=send_sem, recv_sem=recv_sem,
                device_id=(dp, peer), device_id_type=MESH,
            ).start()
            return 0

        lax.fori_loop(1, PEERS, to_peer, 0)

    def many(src, dst, send_sem, recv_sem, count=PEERS - 1):
        return pltpu.make_async_remote_copy(
            src_ref=src.at[pl.ds(0, count)], dst_ref=dst.at[pl.ds(0, count)],
            send_sem=send_sem, recv_sem=recv_sem,
            device_id=(dp, right), device_id_type=MESH,
        )

    def sending(half, c):
        return sent.at[half, c], got.at[half, c], sent_s.at[half, c], got_s.at[half, c]

    def returning(half, c):
        return back_sent.at[half, c], back_got.at[half, c], back_ss.at[half, c], back_rs.at[half, c]

    def kv_copy(c, to_right):
        return pltpu.make_async_remote_copy(
            src_ref=kv.at[c, 1], dst_ref=kv.at[c, 0 if to_right else 2],
            send_sem=kv_ss.at[c, int(to_right)], recv_sem=kv_rs.at[c, int(to_right)],
            device_id=(dp, right if to_right else left), device_id_type=MESH,
        )

    def part_copy(c, to_right):
        side = int(to_right)
        return pltpu.make_async_remote_copy(
            src_ref=part_sent.at[c, side], dst_ref=part_got.at[c, side],
            send_sem=part_ss.at[c, side], recv_sem=part_rs.at[c, side],
            device_id=(dp, right if to_right else left), device_id_type=MESH,
        )

    fill(0, 0)
    pl.semaphore_wait(barrier, PEERS - 1 + PACKS - 1)
    scatter(*sending(0, 0))

    ranked = jnp.where(
        jnp.broadcast_to(rank, (ROWS, ROWS)) == iota((ROWS, ROWS), 0),
        jnp.broadcast_to(slot + 1, (ROWS, ROWS)),
        0,
    ).astype(F32)
    marks = dot_t(to.astype(BF16), ranked.astype(BF16))
    for peer in range(PEERS):
        marks_out[peer] = marks[peer : peer + 1]
    marks_in[me] = marks_out[me]
    scatter(marks_out, marks_in, marks_ss, marks_rs)

    def early(c, _):
        fill(0, c)
        scatter(*sending(0, c))
        return 0

    lax.fori_loop(1, CHUNKS, early, 0)

    for c in range(CHUNKS):
        bias[c] = bias_flat[c * WIDE : (c + 1) * WIDE].reshape(1, WIDE)

    first = me * ROWS
    row_pos = first + iota((ROWS, 3 * ROWS), 0)
    col_pos = first - ROWS + iota((ROWS, 3 * ROWS), 1)
    row_seg = jnp.zeros((ROWS, 3 * ROWS), jnp.int32)
    col_seg = jnp.zeros((ROWS, 3 * ROWS), jnp.int32)
    end = jnp.int32(0)
    for utt in range(4):
        end = end + lengths_ref[0, utt]
        row_seg = row_seg + (row_pos >= end).astype(jnp.int32)
        col_seg = col_seg + (col_pos >= end).astype(jnp.int32)
    alive = (
        (jnp.abs(row_pos - col_pos) <= ROWS)
        & (row_seg == col_seg)
        & (col_pos >= 0)
        & (col_pos < PEERS * ROWS)
    )
    masked = jnp.where(alive, 0.0, -1e30).astype(F32)
    live[0:ROWS] = masked
    live[ROWS:] = masked
    gb[...] = jnp.zeros_like(gb)
    unpack[...] = jnp.transpose(pack[...].astype(F32)).astype(BF16)

    many(marks_out, marks_in, marks_ss, marks_rs).wait_recv()
    arrived = jnp.concatenate([marks_in[peer] for peer in range(PEERS)], axis=0)
    spread = (iota((PAIRS, PEERS), 0) // (2 * ROOM) == iota((PAIRS, PEERS), 1)).astype(BF16)
    copied = dot(spread, arrived.astype(BF16))
    copied = jnp.where(iota((PAIRS, ROWS), 0) % ROOM == iota((PAIRS, ROWS), 1), copied, 0.0)
    mark = jnp.sum(copied, axis=1, keepdims=True).astype(jnp.int32)
    second = iota((PAIRS, 1), 0) % (2 * ROOM) // ROOM
    landing = jnp.where(mark > 0, mark - 1 + ROWS * second, -1)
    lands = (jnp.broadcast_to(landing, (PAIRS, 2 * ROWS)) == iota((PAIRS, 2 * ROWS), 1)).astype(F32)
    unland[...] = lands.astype(BF16)
    land[...] = jnp.transpose(lands).astype(BF16)

    def arrive(half, c):
        many(*sending(half, c)).wait_recv()
        return dot(land[...], got[half, c].reshape(PAIRS, WIDE))

    def arrive_kv(c, _):
        kv[c, 1] = arrive(0, c).astype(BF16)
        kv_copy(c, True).start()
        kv_copy(c, False).start()
        fill(1, c)
        scatter(*sending(1, c))
        return 0

    lax.fori_loop(0, CHUNKS, arrive_kv, 0)

    low = iota((ROWS, LANES), 1) < HEAD_DIM
    scale = 1.0 / HEAD_DIM**0.5

    def stacked(a):
        zero = jnp.zeros_like(a)
        return jnp.concatenate([jnp.where(low, a, zero), jnp.where(low, zero, a)], axis=0)

    def merged(a):
        return jnp.where(low, a[:ROWS], a[ROWS:])

    def two_heads(c, sub):
        lanes = slice(sub * LANES, (sub + 1) * LANES)
        keys = jnp.concatenate([kv[c, side, 0:ROWS, lanes] for side in range(3)], axis=0)
        values = jnp.concatenate([kv[c, side, ROWS:, lanes] for side in range(3)], axis=0)
        b = stacked(y[0:ROWS, lanes]).astype(BF16)
        g32 = stacked(y[ROWS:, lanes])
        g = g32.astype(BF16)
        s = dot_t(b, keys) * scale + live[...]
        top = jnp.max(s, axis=1, keepdims=True)
        e = jnp.exp(s - top)
        p = e * (1.0 / jnp.sum(e, axis=1, keepdims=True))
        prob = p.astype(BF16)
        o = merged(dot(prob, values)).astype(BF16)
        o32 = o.astype(F32)
        delta = jnp.sum(g32 * jnp.concatenate([o32, o32], axis=0), axis=1, keepdims=True)
        ds = (p * (dot_t(g, values) - delta) * scale).astype(BF16)
        dq = merged(dot(ds, keys))
        dk = t_dot(ds, b)
        dv = t_dot(prob, g)
        for side, at in ((0, 0), (1, 2 * ROWS)):
            part_sent[c, side, 0:ROWS, lanes] = dk[at : at + ROWS].astype(BF16)
            part_sent[c, side, ROWS:, lanes] = dv[at : at + ROWS].astype(BF16)
        own_parts[c, 0:ROWS, lanes] = dk[ROWS : 2 * ROWS]
        own_parts[c, ROWS:, lanes] = dv[ROWS : 2 * ROWS]
        result[0:ROWS, lanes] = o
        result[ROWS:, lanes] = dq.astype(BF16)
        gb[pl.ds(2 * c + sub, 1), :] = jnp.sum(dq, axis=0, keepdims=True)

    def give_back(half, c, rows):
        back_sent[half, c] = dot(unland[...], rows).astype(BF16).reshape(PEERS, 2 * ROOM, WIDE)
        back_got[half, c, me] = back_sent[half, c, me]
        scatter(*returning(half, c))

    def give_parts(c):
        part_copy(c, True).wait_recv()
        part_copy(c, False).wait_recv()
        total = own_parts[c] + part_got[c, 0].astype(F32) + part_got[c, 1].astype(F32)
        give_back(1, c, total.astype(BF16))

    def share_packs(o, _):
        peer = lax.rem(dp + o, PACKS)
        pltpu.make_async_remote_copy(
            src_ref=gb, dst_ref=gb_dp.at[dp],
            send_sem=dp_ss, recv_sem=dp_rs,
            device_id=(peer, me), device_id_type=MESH,
        ).start()
        return 0

    def attend(c, _):
        qg = arrive(1, c)
        y[0:ROWS] = (qg[:ROWS] + bias[c]).astype(BF16).astype(F32)
        y[ROWS:] = qg[ROWS:]
        kv_copy(c, True).wait_recv()
        kv_copy(c, False).wait_recv()
        two_heads(c, 0)
        two_heads(c, 1)
        part_copy(c, True).start()
        part_copy(c, False).start()

        @pl.when(c == CHUNKS - 1)
        def _():
            gb_dp[dp] = gb[...]
            lax.fori_loop(1, PACKS, share_packs, 0)

        give_back(0, c, result[...])

        @pl.when(c >= 1)
        def _():
            give_parts(c - 1)

        return 0

    lax.fori_loop(0, CHUNKS, attend, 0)

    many(gb_dp, gb_dp, dp_ss, dp_rs, PACKS - 1).wait_recv()
    gb_packs[...] = jnp.sum(gb_dp[...], axis=0)
    gb_seq[me] = gb_packs[...]

    def share_seq(o, _):
        peer = lax.rem(me + o, PEERS)
        pltpu.make_async_remote_copy(
            src_ref=gb_packs, dst_ref=gb_seq.at[me],
            send_sem=seq_ss, recv_sem=seq_rs,
            device_id=(dp, peer), device_id_type=MESH,
        ).start()
        return 0

    lax.fori_loop(1, PEERS, share_seq, 0)
    give_parts(CHUNKS - 1)

    outputs = ((o_hbm, dq_hbm), (dk_hbm, dv_hbm))

    def store(half, row, c):
        return pltpu.make_async_copy(
            x.at[half, c, pl.ds(row * ROWS, ROWS)],
            outputs[half][row].at[:, wide(c)],
            out_s.at[half, row, c],
        )

    def finish(half, c):
        many(*returning(half, c)).wait_recv()
        x[half, c] = dot(unpack[...], back_got[half, c].reshape(PAIRS, WIDE)).astype(BF16)
        store(half, 0, c).start()
        store(half, 1, c).start()

    def finish_both(c, _):
        finish(0, c)
        finish(1, c)
        return 0

    lax.fori_loop(0, CHUNKS - 1, finish_both, 0)
    finish(0, CHUNKS - 1)
    many(gb_seq, gb_seq, seq_ss, seq_rs).wait_recv()
    total = jnp.sum(gb_seq[...], axis=0)
    for part in range(WIDTH // LANES):
        gb_out[:, part * LANES : (part + 1) * LANES] = total[part : part + 1]

    many(marks_out, marks_in, marks_ss, marks_rs).wait_send()
    many(gb_dp, gb_dp, dp_ss, dp_rs, PACKS - 1).wait_send()
    many(gb_seq, gb_seq, seq_ss, seq_rs).wait_send()

    def left_all(c, _):
        for half in range(2):
            many(*sending(half, c)).wait_send()
            many(*returning(half, c)).wait_send()
            kv_copy(c, half == 0).wait_send()
            part_copy(c, half == 0).wait_send()
        return 0

    lax.fori_loop(0, CHUNKS, left_all, 0)
    finish(1, CHUNKS - 1)

    def stored(c, _):
        for half in range(2):
            for row in range(2):
                store(half, row, c).wait()
        return 0

    lax.fori_loop(0, CHUNKS, stored, 0)


def copies(*refs):
    source, target, held = refs[0:5], refs[5:10], refs[10:15]
    flat, in_s, out_s = refs[15:]
    loads = [pltpu.make_async_copy(source[i], held[i], in_s.at[i]) for i in range(5)]
    stores = [pltpu.make_async_copy(held[i], target[i], out_s.at[i]) for i in range(4)]
    stores.append(pltpu.make_async_copy(flat, target[4], out_s.at[4]))
    for load in loads:
        load.start()
    for i in (4, 0, 1, 2, 3):
        loads[i].wait()
        if i == 4:
            flat[...] = held[4][...].reshape(WIDTH)
        stores[i].start()
    for store in stores:
        store.wait()


def body(queries, keys, values, cotangent, pos_bias, owner, slot, lengths):
    vmem = pl.BlockSpec(memory_space=pltpu.VMEM)
    hbm = pl.BlockSpec(memory_space=pltpu.HBM)
    rows = jax.ShapeDtypeStruct((ROWS, WIDTH), BF16)
    bias = jax.ShapeDtypeStruct((1, WIDTH), F32)
    dma = pltpu.SemaphoreType.DMA
    block = (2, CHUNKS, PEERS, 2 * ROOM, WIDE)
    sides = (CHUNKS, 2, 2 * ROWS, WIDE)
    results = pl.pallas_call(
        kernel,
        out_shape=(rows, rows, rows, rows, bias),
        in_specs=[hbm] * 8,
        out_specs=(hbm,) * 4 + (vmem,),
        scratch_shapes=[
            pltpu.VMEM((2, CHUNKS, 2 * ROWS, WIDE), BF16),
            pltpu.VMEM((2 * ROWS, WIDE), F32),
            pltpu.VMEM((PAIRS, 2 * ROWS), BF16),
            pltpu.VMEM((2 * ROWS, PAIRS), BF16),
            pltpu.VMEM((2 * ROWS, PAIRS), BF16),
            pltpu.VMEM((PAIRS, 2 * ROWS), BF16),
            pltpu.VMEM((2 * ROWS, 3 * ROWS), F32),
            pltpu.VMEM((PEERS, 1, LANES), F32),
            pltpu.VMEM((PEERS, 1, LANES), F32),
            pltpu.VMEM(block, BF16),
            pltpu.VMEM(block, BF16),
            pltpu.VMEM(block, BF16),
            pltpu.VMEM(block, BF16),
            pltpu.VMEM((CHUNKS, 3, 2 * ROWS, WIDE), BF16),
            pltpu.VMEM(sides, BF16),
            pltpu.VMEM(sides, BF16),
            pltpu.VMEM((CHUNKS, 2 * ROWS, WIDE), F32),
            pltpu.VMEM((2 * ROWS, WIDE), BF16),
            pltpu.VMEM((8, LANES), F32),
            pltpu.VMEM((PACKS, 8, LANES), F32),
            pltpu.VMEM((8, LANES), F32),
            pltpu.VMEM((PEERS, 8, LANES), F32),
            pltpu.VMEM((WIDTH,), F32),
            pltpu.VMEM((CHUNKS, 1, WIDE), F32),
            pltpu.VMEM((1, ROWS), jnp.int32),
            pltpu.VMEM((1, ROWS), jnp.int32),
            pltpu.SMEM((1, 4), jnp.int32),
            dma((4,)), dma((4, CHUNKS)), dma((2, 2, CHUNKS)),
            dma, dma,
            dma((2, CHUNKS)), dma((2, CHUNKS)), dma((2, CHUNKS)), dma((2, CHUNKS)),
            dma((CHUNKS, 2)), dma((CHUNKS, 2)), dma((CHUNKS, 2)), dma((CHUNKS, 2)),
            dma, dma, dma, dma,
        ],
        compiler_params=pltpu.CompilerParams(
            collective_id=0, has_side_effects=True, vmem_limit_bytes=60 << 20
        ),
    )(
        queries[0], keys[0], values[0], cotangent[0],
        pos_bias, owner, slot, lengths,
    )
    o, dq, dk, dv, gb = pl.pallas_call(
        copies,
        out_shape=(rows, rows, rows, rows, jax.ShapeDtypeStruct((WIDTH,), F32)),
        in_specs=[hbm] * 5,
        out_specs=(hbm,) * 5,
        scratch_shapes=[pltpu.VMEM((ROWS, WIDTH), BF16)] * 4
        + [pltpu.VMEM((1, WIDTH), F32), pltpu.VMEM((WIDTH,), F32), dma((5,)), dma((5,))],
        compiler_params=pltpu.CompilerParams(vmem_limit_bytes=60 << 20),
    )(*results)
    return o[None], dq[None], dk[None], dv[None], gb


def solution(mesh):
    rows = P("dp", "seq", None)
    in_specs = (rows, rows, rows, rows, P(), P("dp", "seq"), P("dp", "seq"), P("dp", None))
    out_specs = (rows, rows, rows, rows, P())
    return jax.shard_map(body, mesh=mesh, in_specs=in_specs, out_specs=out_specs, check_vma=False)
```

```python
import jax
import jax.numpy as jnp
from jax import lax
from jax.experimental import pallas as pl
from jax.experimental.pallas import tpu as pltpu
from jax.sharding import PartitionSpec as P

HEADS = 12
HEAD_DIM = 64
ROWS = 128
WIDTH = HEADS * HEAD_DIM
LANES = 128
WIDE = 256
PAIRS = HEADS // 2
CHIPS = 16
PEERS = 32
PACKS = 16
FRAMES = PEERS * ROWS
HALF = FRAMES // 2
BASE = HALF - 2 * ROWS
HELD = HALF + 2 * ROWS
TALL = 256
GROUP = 4
MESH = pl.DeviceIdType.MESH
BF16 = jnp.bfloat16
F32 = jnp.float32


def dot(a, b):
    return jnp.dot(a, b, preferred_element_type=F32)


def dot_t(a, b):
    return lax.dot_general(a, b, (((1,), (1,)), ((), ())), preferred_element_type=F32)


def t_dot(a, b):
    return lax.dot_general(a, b, (((0,), (0,)), ((), ())), preferred_element_type=F32)


def iota(shape, dim):
    return lax.broadcasted_iota(jnp.int32, shape, dim)


def far_first(j):
    return lax.rem(CHIPS // 2 + (j + 1) // 2 * (2 * lax.rem(j, 2) - 1), CHIPS)


def chip_of(head):
    return head // 3 * 4 + head % 3


def kernel(
    q_hbm, k_hbm, v_hbm, g_hbm, bias_hbm, owner_hbm, slot_hbm, lengths_hbm,
    o_hbm, dq_hbm, dk_hbm, dv_hbm, gb_out,
    x, y, blocks, got, pos_out, pos_in, pos_row, pos_col,
    held, band, res, dkv, results, part_out, part_in, ret, back,
    bias_flat, bias, owner_ref, slot_ref, lengths_ref,
    gb, gb_dp, gb_packs, gb_seq,
    small_s, in_s, out_s,
    blocks_ss, got_rs, pos_ss, pos_rs, relay_ss, relay_rs,
    part_ss, part_rs, ret_ss, back_rs, seq_ss, seq_rs, dp_ss, dp_rs,
):
    dp = lax.axis_index("dp")
    me = lax.axis_index("seq")
    chip = me // 2
    core = lax.rem(me, 2)
    sibling = me + 1 - 2 * core
    active = lax.rem(chip, 4) < 3
    my_head = jnp.minimum(chip // 4 * 3 + lax.rem(chip, 4), HEADS - 1)

    barrier = pltpu.get_barrier_semaphore()

    def greet_seq(o, _):
        peer = lax.rem(me + o, PEERS)
        pl.semaphore_signal(barrier, inc=1, device_id=(dp, peer), device_id_type=MESH)
        return 0

    def greet_dp(o, _):
        peer = lax.rem(dp + o, PACKS)
        pl.semaphore_signal(barrier, inc=1, device_id=(peer, me), device_id_type=MESH)
        return 0

    lax.fori_loop(1, PEERS, greet_seq, 0)
    lax.fori_loop(1, PACKS, greet_dp, 0)

    inputs = (q_hbm, g_hbm, k_hbm, v_hbm)
    loads = [pltpu.make_async_copy(inputs[i], x.at[i], in_s.at[i]) for i in range(4)]
    small = [
        pltpu.make_async_copy(src, dst, small_s.at[i])
        for i, (src, dst) in enumerate(
            [
                (owner_hbm, owner_ref),
                (slot_hbm, slot_ref),
                (bias_hbm, bias_flat),
                (lengths_hbm, lengths_ref),
            ]
        )
    ]
    for copy in small + loads:
        copy.start()
    for copy in small:
        copy.wait()
    pos_out[...] = owner_ref[...] * ROWS + slot_ref[...]

    low = iota((ROWS, LANES), 1) < HEAD_DIM

    def swapped(a):
        return pltpu.roll(a, HEAD_DIM, 1)

    for copy in loads:
        copy.wait()
    for pair in range(PAIRS):
        lanes = slice(pair * LANES, (pair + 1) * LANES)
        q, g, k, v = (x[i, :, lanes].astype(F32) for i in range(4))
        for at, (a, b) in ((0, (q, g)), (LANES, (k, v))):
            blocks[2 * pair, :, at : at + LANES] = jnp.where(low, a, swapped(b)).astype(BF16)
            blocks[2 * pair + 1, :, at : at + LANES] = jnp.where(low, swapped(a), b).astype(BF16)

    def send_copy(head, j, peer):
        return pltpu.make_async_remote_copy(
            src_ref=blocks.at[head], dst_ref=got.at[j, core],
            send_sem=blocks_ss.at[j], recv_sem=got_rs.at[j],
            device_id=(dp, peer), device_id_type=MESH,
        )

    def relay_copy(j, part):
        return pltpu.make_async_remote_copy(
            src_ref=got.at[j, part], dst_ref=got.at[j, part],
            send_sem=relay_ss.at[j], recv_sem=relay_rs.at[j],
            device_id=(dp, sibling), device_id_type=MESH,
        )

    def part_copy(j):
        return pltpu.make_async_remote_copy(
            src_ref=part_out.at[j], dst_ref=part_in.at[j],
            send_sem=part_ss.at[j], recv_sem=part_rs.at[j],
            device_id=(dp, sibling), device_id_type=MESH,
        )

    def ret_copy(j, head, peer):
        return pltpu.make_async_remote_copy(
            src_ref=ret.at[j], dst_ref=back.at[head],
            send_sem=ret_ss.at[j], recv_sem=back_rs.at[head],
            device_id=(dp, peer), device_id_type=MESH,
        )

    def many(buf, send_sem, recv_sem, count):
        return pltpu.make_async_remote_copy(
            src_ref=buf.at[pl.ds(0, count)], dst_ref=buf.at[pl.ds(0, count)],
            send_sem=send_sem, recv_sem=recv_sem,
            device_id=(dp, sibling), device_id_type=MESH,
        )

    pl.semaphore_wait(barrier, PEERS - 1 + PACKS - 1)

    def send_pos(j, _):
        to = lax.rem(chip + far_first(j), CHIPS)

        def one(peer):
            pltpu.make_async_remote_copy(
                src_ref=pos_out, dst_ref=pos_in.at[2 * j + core],
                send_sem=pos_ss, recv_sem=pos_rs,
                device_id=(dp, peer), device_id_type=MESH,
            ).start()

        @pl.when(j < CHIPS - 1)
        def _():
            one(2 * to)
            one(2 * to + 1)

        @pl.when(j == CHIPS - 1)
        def _():
            one(sibling)

        return 0

    lax.fori_loop(0, CHIPS, send_pos, 0)
    pos_in[2 * CHIPS - 2 + core] = pos_out[...]

    def target(j):
        to = lax.rem(chip + far_first(j), CHIPS)
        return to, lax.rem(to, 4) < 3, jnp.minimum(to // 4 * 3 + lax.rem(to, 4), HEADS - 1)

    def send(j, _):
        to, has_head, head = target(j)

        @pl.when(has_head)
        def _():
            send_copy(head, j, 2 * to + core).start()

        return 0

    lax.fori_loop(0, CHIPS - 1, send, 0)

    many(pos_in, pos_ss, pos_rs, PEERS - 1).wait_recv()
    first = core * BASE

    @pl.when(active)
    def _():
        got[CHIPS - 1, core] = blocks[my_head]
        held[0:ROWS] = jnp.zeros((ROWS, WIDE), BF16)
        held[ROWS + HELD :] = jnp.zeros((ROWS, WIDE), BF16)
        dkv[...] = jnp.zeros_like(dkv)
        places = jnp.concatenate([pos_in[i] for i in range(PEERS)], axis=0)
        for i in range(PEERS // 8):
            pos_row[i] = jnp.concatenate([pos_in[8 * i + n] for n in range(8)], axis=1)
        pos_col[...] = jnp.transpose(
            jnp.concatenate([places, jnp.zeros((ROWS - PEERS, ROWS), jnp.int32)], axis=0).astype(F32)
        ).astype(jnp.int32)
        apart = iota((ROWS, 3 * ROWS), 0) - iota((ROWS, 3 * ROWS), 1) + ROWS
        band[...] = jnp.where(jnp.abs(apart) <= ROWS, 0.0, -1e30).astype(F32)
        for pair in range(PAIRS):
            bias[pair] = bias_flat[pair * LANES : (pair + 1) * LANES].reshape(1, LANES)

        def group(n, _):
            def take(j, _):
                @pl.when(j < CHIPS - 1)
                def _():
                    send_copy(0, j, sibling).wait_recv()

                relay_copy(j, core).start()
                return 0

            def taken(j, _):
                relay_copy(j, 1 - core).wait_recv()
                return 0

            lax.fori_loop(GROUP * n, GROUP * (n + 1), take, 0)
            lax.fori_loop(GROUP * n, GROUP * (n + 1), taken, 0)
            rows = got[pl.ds(GROUP * n, GROUP)].reshape(2 * GROUP * ROWS, WIDE)
            there = pos_row[n] - first

            def place(m, _):
                shape = (TALL, 2 * GROUP * ROWS)
                chosen = (jnp.broadcast_to(there - m * TALL, shape) == iota(shape, 0)).astype(F32)
                found = dot(chosen.astype(BF16), rows)
                at = pl.ds(pl.multiple_of(ROWS + m * TALL, ROWS), TALL)

                @pl.when(n == 0)
                def _():
                    held[at] = found.astype(BF16)

                @pl.when(n > 0)
                def _():
                    held[at] = (held[at].astype(F32) + found).astype(BF16)

                return 0

            lax.fori_loop(0, HELD // TALL, place, 0)
            return 0

        lax.fori_loop(0, CHIPS // GROUP, group, 0)

        pair_bias = bias[my_head // 2]
        head_bias = jnp.where(lax.rem(my_head, 2) == 1, swapped(pair_bias), pair_bias)
        head_bias = jnp.where(low[0:1], head_bias, 0.0)
        scale = 1.0 / HEAD_DIM**0.5

        def segment(pos):
            seg = jnp.zeros_like(pos)
            end = jnp.int32(0)
            for utt in range(4):
                end = end + lengths_ref[0, utt]
                seg = seg + (pos >= end).astype(jnp.int32)
            return seg

        def attend(i, total):
            start = pl.multiple_of((core + i) * ROWS, ROWS)
            at = pl.ds(pl.multiple_of(start + ROWS, ROWS), ROWS)
            window = pl.ds(start, 3 * ROWS)
            here = first + start
            row_pos = here + iota((ROWS, 1), 0)
            col_pos = here - ROWS + iota((1, 3 * ROWS), 1)
            row_seg = segment(row_pos)
            col_seg = jnp.where((col_pos >= 0) & (col_pos < FRAMES), segment(col_pos), -1)
            bg = (held[at, 0:LANES].astype(F32) + head_bias).astype(BF16).astype(F32)
            kv = held[window, LANES:]
            both = jnp.concatenate([jnp.where(low, bg, 0.0), jnp.where(low, 0.0, bg)], axis=0).astype(BF16)
            product = dot_t(both, kv)
            s = jnp.where(row_seg == col_seg, product[:ROWS] * scale + band[...], -1e30)
            top = jnp.max(s, axis=1, keepdims=True)
            e = jnp.exp(s - top)
            p = e * (1.0 / jnp.sum(e, axis=1, keepdims=True))
            prob = p.astype(BF16)
            o = dot(prob, kv).astype(BF16).astype(F32)
            delta = jnp.sum(jnp.where(low, 0.0, bg * o), axis=1, keepdims=True)
            ds = (p * (product[ROWS:] - delta) * scale).astype(BF16)
            dq = dot(ds, kv)
            res[at] = jnp.where(low, dq, o).astype(BF16)
            dkv[window] += t_dot(jnp.concatenate([ds, prob], axis=0), both)
            mine = (i + core >= 2 * core) & (i + core < HALF // ROWS + 2 * core)
            return total + jnp.where(mine, jnp.sum(dq, axis=0, keepdims=True), 0.0)

        gb[...] = lax.fori_loop(0, HALF // ROWS + 1, attend, jnp.zeros((1, LANES), F32))
        own = pl.ds(pl.multiple_of(ROWS + 2 * ROWS * core, ROWS), HALF)
        results[:, 0:LANES] = res[own]
        results[:, LANES:] = dkv[own].astype(BF16)

    @pl.when(jnp.logical_not(active))
    def _():
        gb[...] = jnp.zeros_like(gb)

    gb_dp[dp] = gb[...]

    def share_dp(o, _):
        peer = lax.rem(dp + o, PACKS)
        pltpu.make_async_remote_copy(
            src_ref=gb, dst_ref=gb_dp.at[dp],
            send_sem=dp_ss, recv_sem=dp_rs,
            device_id=(peer, me), device_id_type=MESH,
        ).start()
        return 0

    lax.fori_loop(1, PACKS, share_dp, 0)

    def source(j):
        return lax.rem(chip - far_first(j) + CHIPS, CHIPS)

    def make_parts(j):
        own_first = core * HALF
        lane = iota((ROWS, LANES), 1)
        cols = [
            jnp.sum(jnp.where(lane == 2 * j + n, pos_col[...], 0), axis=1, keepdims=True) - own_first
            for n in range(2)
        ]
        col = jnp.concatenate(cols, axis=0)
        shape = (2 * ROWS, HALF)
        chosen = (jnp.broadcast_to(col, shape) == iota(shape, 1)).astype(F32).astype(BF16)
        y[...] = dot(chosen, results[...]).astype(BF16)
        part_out[j] = y[pl.ds(pl.multiple_of((1 - core) * ROWS, ROWS), ROWS)]
        ret[j] = y[pl.ds(pl.multiple_of(core * ROWS, ROWS), ROWS)]
        part_copy(j).start()

    def give_back(j):
        part_copy(j).wait_recv()
        ret[j] = (ret[j].astype(F32) + part_in[j].astype(F32)).astype(BF16)

        @pl.when(j < CHIPS - 1)
        def _():
            ret_copy(j, my_head, 2 * source(j) + core).start()

        @pl.when(j == CHIPS - 1)
        def _():
            back[my_head] = ret[j]

    @pl.when(active)
    def _():
        def step(j, _):
            @pl.when(j < CHIPS)
            def _():
                make_parts(j)

            @pl.when(j >= 1)
            def _():
                give_back(j - 1)

            return 0

        lax.fori_loop(0, CHIPS + 1, step, 0)

    many(gb_dp, dp_ss, dp_rs, PACKS - 1).wait_recv()
    gb_packs[...] = jnp.sum(gb_dp[...], axis=0)
    gb_seq[me] = gb_packs[...]

    def share_seq(o, _):
        peer = lax.rem(me + o, PEERS)
        pltpu.make_async_remote_copy(
            src_ref=gb_packs, dst_ref=gb_seq.at[me],
            send_sem=seq_ss, recv_sem=seq_rs,
            device_id=(dp, peer), device_id_type=MESH,
        ).start()
        return 0

    lax.fori_loop(1, PEERS, share_seq, 0)

    outputs = (dq_hbm, o_hbm, dk_hbm, dv_hbm)

    def store(array, pair):
        lanes = slice(pair * LANES, (pair + 1) * LANES)
        return pltpu.make_async_copy(
            x.at[array, :, lanes], outputs[array].at[:, lanes], out_s.at[array, pair]
        )

    for pair in range(PAIRS):
        for head in (2 * pair, 2 * pair + 1):

            @pl.when(chip != chip_of(head))
            def _():
                ret_copy(0, head, sibling).wait_recv()

        lanes = slice(pair * LANES, (pair + 1) * LANES)
        for n in range(2):
            a = back[2 * pair, :, n * LANES : (n + 1) * LANES].astype(F32)
            b = back[2 * pair + 1, :, n * LANES : (n + 1) * LANES].astype(F32)
            x[2 * n, :, lanes] = jnp.where(low, a, swapped(b)).astype(BF16)
            x[2 * n + 1, :, lanes] = jnp.where(low, swapped(a), b).astype(BF16)
        for array in range(4):
            store(array, pair).start()

    many(gb_seq, seq_ss, seq_rs, PEERS - 1).wait_recv()
    for pair in range(PAIRS):
        a, b = (
            gb_seq[2 * chip_of(head)] + gb_seq[2 * chip_of(head) + 1]
            for head in (2 * pair, 2 * pair + 1)
        )
        gb_out[:, pair * LANES : (pair + 1) * LANES] = jnp.where(low[0:1], a, swapped(b))

    many(pos_in, pos_ss, pos_rs, PEERS - 1).wait_send()
    many(gb_dp, dp_ss, dp_rs, PACKS - 1).wait_send()
    many(gb_seq, seq_ss, seq_rs, PEERS - 1).wait_send()

    def left(j, _):
        to, has_head, head = target(j)

        @pl.when(has_head & (j < CHIPS - 1))
        def _():
            send_copy(head, j, 2 * to + core).wait_send()

        @pl.when(active)
        def _():
            relay_copy(j, core).wait_send()
            part_copy(j).wait_send()

            @pl.when(j < CHIPS - 1)
            def _():
                ret_copy(j, my_head, 2 * source(j) + core).wait_send()

        return 0

    lax.fori_loop(0, CHIPS, left, 0)
    for pair in range(PAIRS):
        for array in range(4):
            store(array, pair).wait()


def copies(*refs):
    source, target, held = refs[0:5], refs[5:10], refs[10:15]
    flat, in_s, out_s = refs[15:]
    loads = [pltpu.make_async_copy(source[i], held[i], in_s.at[i]) for i in range(5)]
    stores = [pltpu.make_async_copy(held[i], target[i], out_s.at[i]) for i in range(4)]
    stores.append(pltpu.make_async_copy(flat, target[4], out_s.at[4]))
    for load in loads:
        load.start()
    for i in (4, 0, 1, 2, 3):
        loads[i].wait()
        if i == 4:
            flat[...] = held[4][...].reshape(WIDTH)
        stores[i].start()
    for move in stores:
        move.wait()


def body(queries, keys, values, cotangent, pos_bias, owner, slot, lengths):
    vmem = pl.BlockSpec(memory_space=pltpu.VMEM)
    hbm = pl.BlockSpec(memory_space=pltpu.HBM)
    rows = jax.ShapeDtypeStruct((ROWS, WIDTH), BF16)
    row = jax.ShapeDtypeStruct((1, WIDTH), F32)
    dma = pltpu.SemaphoreType.DMA
    i32 = jnp.int32
    results = pl.pallas_call(
        kernel,
        out_shape=(rows, rows, rows, rows, row),
        in_specs=[hbm] * 8,
        out_specs=(hbm,) * 4 + (vmem,),
        scratch_shapes=[
            pltpu.VMEM((4, ROWS, WIDTH), BF16),
            pltpu.VMEM((2 * ROWS, WIDE), BF16),
            pltpu.VMEM((HEADS, ROWS, WIDE), BF16),
            pltpu.VMEM((CHIPS, 2, ROWS, WIDE), BF16),
            pltpu.VMEM((1, ROWS), i32),
            pltpu.VMEM((PEERS, 1, ROWS), i32),
            pltpu.VMEM((PEERS // 8, 1, 8 * ROWS), i32),
            pltpu.VMEM((ROWS, LANES), i32),
            pltpu.VMEM((HELD + 2 * ROWS, WIDE), BF16),
            pltpu.VMEM((ROWS, 3 * ROWS), F32),
            pltpu.VMEM((HELD + 2 * ROWS, LANES), BF16),
            pltpu.VMEM((HELD + 2 * ROWS, LANES), F32),
            pltpu.VMEM((HALF, WIDE), BF16),
            pltpu.VMEM((CHIPS, ROWS, WIDE), BF16),
            pltpu.VMEM((CHIPS, ROWS, WIDE), BF16),
            pltpu.VMEM((CHIPS, ROWS, WIDE), BF16),
            pltpu.VMEM((HEADS, ROWS, WIDE), BF16),
            pltpu.VMEM((WIDTH,), F32),
            pltpu.VMEM((PAIRS, 1, LANES), F32),
            pltpu.VMEM((1, ROWS), i32),
            pltpu.VMEM((1, ROWS), i32),
            pltpu.SMEM((1, 4), i32),
            pltpu.VMEM((1, LANES), F32),
            pltpu.VMEM((PACKS, 1, LANES), F32),
            pltpu.VMEM((1, LANES), F32),
            pltpu.VMEM((PEERS, 1, LANES), F32),
            dma((4,)), dma((4,)), dma((4, PAIRS)),
            dma((CHIPS,)), dma((CHIPS,)), dma, dma, dma((CHIPS,)), dma((CHIPS,)),
            dma((CHIPS,)), dma((CHIPS,)), dma((CHIPS,)), dma((HEADS,)),
            dma, dma, dma, dma,
        ],
        compiler_params=pltpu.CompilerParams(
            collective_id=0, has_side_effects=True, vmem_limit_bytes=60 << 20
        ),
    )(
        queries[0], keys[0], values[0], cotangent[0],
        pos_bias, owner, slot, lengths,
    )
    o, dq, dk, dv, gb = pl.pallas_call(
        copies,
        out_shape=(rows, rows, rows, rows, jax.ShapeDtypeStruct((WIDTH,), F32)),
        in_specs=[hbm] * 5,
        out_specs=(hbm,) * 5,
        scratch_shapes=[pltpu.VMEM((ROWS, WIDTH), BF16)] * 4
        + [pltpu.VMEM((1, WIDTH), F32), pltpu.VMEM((WIDTH,), F32), dma((5,)), dma((5,))],
        compiler_params=pltpu.CompilerParams(vmem_limit_bytes=60 << 20),
    )(*results)
    return o[None], dq[None], dk[None], dv[None], gb


def solution(mesh):
    rows = P("dp", "seq", None)
    in_specs = (rows, rows, rows, rows, P(), P("dp", "seq"), P("dp", "seq"), P("dp", None))
    out_specs = (rows, rows, rows, rows, P())
    return jax.shard_map(body, mesh=mesh, in_specs=in_specs, out_specs=out_specs, check_vma=False)
```

```python
import jax
import jax.numpy as jnp
from jax import lax
from jax.experimental import pallas as pl
from jax.experimental.pallas import tpu as pltpu
from jax.sharding import PartitionSpec as P

HEADS = 12
HEAD_DIM = 64
ROWS = 128
WIDTH = HEADS * HEAD_DIM
LANES = 128
WIDE = 256
PAIRS = HEADS // 2
CHIPS = 16
PEERS = 32
PACKS = 16
FRAMES = PEERS * ROWS
HALF = FRAMES // 2
BASE = HALF - 2 * ROWS
HELD = HALF + 2 * ROWS
TALL = 256
GROUP = 4
SELF = 1
MESH = pl.DeviceIdType.MESH
BF16 = jnp.bfloat16
F32 = jnp.float32


def dot(a, b):
    return jnp.dot(a, b, preferred_element_type=F32)


def dot_t(a, b):
    return lax.dot_general(a, b, (((1,), (1,)), ((), ())), preferred_element_type=F32)


def t_dot(a, b):
    return lax.dot_general(a, b, (((0,), (0,)), ((), ())), preferred_element_type=F32)


def iota(shape, dim):
    return lax.broadcasted_iota(jnp.int32, shape, dim)


def wrapped(at, size):
    return jnp.where(at >= size, at - size, at)


def offset(group, at):
    return (8, CHIPS, 1, 9)[at] + (-1, -1, 1, 1)[at] * group


def chip_of(head):
    return head // 3 * 4 + head % 3


def kernel(
    q_hbm, k_hbm, v_hbm, g_hbm, bias_hbm, owner_hbm, slot_hbm, lengths_hbm,
    o_hbm, dq_hbm, dk_hbm, dv_hbm, gb_out,
    x, y, blocks, got, pos_out, pos_in, pos_col,
    held, band, res, dkv, results, part_out, part_in, ret, back,
    bias_flat, bias, owner_ref, slot_ref, lengths_ref,
    gb, gb_dp, gb_half, gb_other, gb_head, gb_heads,
    small_s, in_s, out_s,
    blocks_ss, got_rs, pos_ss, pos_rs, relay_ss, relay_rs,
    part_ss, part_rs, ret_ss, back_rs, heads_ss, heads_rs, dp_ss, dp_rs,
    relay_pos_ss, relay_pos_rs, half_ss, half_rs,
):
    dp = lax.axis_index("dp")
    me = lax.axis_index("seq")
    chip = me // 2
    core = lax.rem(me, 2)
    sibling = me + 1 - 2 * core
    active = lax.rem(chip, 4) < 3
    my_head = jnp.minimum(chip // 4 * 3 + lax.rem(chip, 4), HEADS - 1)

    barrier = pltpu.get_barrier_semaphore()

    def greet_seq(o, _):
        peer = lax.rem(me + o, PEERS)
        pl.semaphore_signal(barrier, inc=1, device_id=(dp, peer), device_id_type=MESH)
        return 0

    def greet_dp(o, _):
        peer = lax.rem(dp + o, PACKS)
        pl.semaphore_signal(barrier, inc=1, device_id=(peer, me), device_id_type=MESH)
        return 0

    lax.fori_loop(1, PEERS, greet_seq, 0)
    lax.fori_loop(1, PACKS, greet_dp, 0)

    inputs = (q_hbm, g_hbm, k_hbm, v_hbm)
    loads = [pltpu.make_async_copy(inputs[i], x.at[i], in_s.at[i]) for i in range(4)]
    small = [
        pltpu.make_async_copy(src, dst, small_s.at[i])
        for i, (src, dst) in enumerate(
            [
                (owner_hbm, owner_ref),
                (slot_hbm, slot_ref),
                (bias_hbm, bias_flat),
                (lengths_hbm, lengths_ref),
            ]
        )
    ]
    for copy in small + loads:
        copy.start()
    for copy in small:
        copy.wait()
    pos_out[...] = owner_ref[...] * ROWS + slot_ref[...]

    low = iota((ROWS, LANES), 1) < HEAD_DIM

    def swapped(a):
        return pltpu.roll(a, HEAD_DIM, 1)

    for copy in loads:
        copy.wait()
    for pair in range(PAIRS):
        lanes = slice(pair * LANES, (pair + 1) * LANES)
        q, g, k, v = (x[i, :, lanes].astype(F32) for i in range(4))
        for at, (a, b) in ((0, (q, g)), (LANES, (k, v))):
            blocks[2 * pair, :, at : at + LANES] = jnp.where(low, a, swapped(b)).astype(BF16)
            blocks[2 * pair + 1, :, at : at + LANES] = jnp.where(low, swapped(a), b).astype(BF16)

    def send_copy(head, j, peer):
        return pltpu.make_async_remote_copy(
            src_ref=blocks.at[head], dst_ref=got.at[core, j],
            send_sem=blocks_ss.at[j], recv_sem=got_rs.at[j],
            device_id=(dp, peer), device_id_type=MESH,
        )

    def relay_copy(j, part):
        return pltpu.make_async_remote_copy(
            src_ref=got.at[part, j], dst_ref=got.at[part, j],
            send_sem=relay_ss.at[j], recv_sem=relay_rs.at[j],
            device_id=(dp, sibling), device_id_type=MESH,
        )

    def part_copy(j):
        return pltpu.make_async_remote_copy(
            src_ref=part_out.at[j], dst_ref=part_in.at[j],
            send_sem=part_ss.at[j], recv_sem=part_rs.at[j],
            device_id=(dp, sibling), device_id_type=MESH,
        )

    def ret_copy(j, head, peer):
        return pltpu.make_async_remote_copy(
            src_ref=ret.at[j], dst_ref=back.at[head],
            send_sem=ret_ss.at[j], recv_sem=back_rs.at[head],
            device_id=(dp, peer), device_id_type=MESH,
        )

    def many(buf, send_sem, recv_sem, count):
        return pltpu.make_async_remote_copy(
            src_ref=buf.at[pl.ds(0, count)], dst_ref=buf.at[pl.ds(0, count)],
            send_sem=send_sem, recv_sem=recv_sem,
            device_id=(dp, sibling), device_id_type=MESH,
        )

    pl.semaphore_wait(barrier, PEERS - 1 + PACKS - 1)

    def pos_copy(j, peer):
        return pltpu.make_async_remote_copy(
            src_ref=pos_out, dst_ref=pos_in.at[core, j],
            send_sem=pos_ss.at[j], recv_sem=pos_rs.at[j],
            device_id=(dp, peer), device_id_type=MESH,
        )

    def relay_pos(n, part):
        rows = pl.ds(GROUP * n, GROUP)
        return pltpu.make_async_remote_copy(
            src_ref=pos_in.at[part, rows], dst_ref=pos_in.at[part, rows],
            send_sem=relay_pos_ss.at[n], recv_sem=relay_pos_rs.at[n],
            device_id=(dp, sibling), device_id_type=MESH,
        )

    half_copy = pltpu.make_async_remote_copy(
        src_ref=gb_half, dst_ref=gb_other,
        send_sem=half_ss, recv_sem=half_rs,
        device_id=(dp, sibling), device_id_type=MESH,
    )

    eighth = lax.rem(chip, 8)

    def each_sent(turn, act, begin=0, end=CHIPS):
        for j in range(begin, end):
            if j == SELF:
                continue
            off = offset(j // GROUP, j % GROUP) % CHIPS
            to = wrapped(chip + off, CHIPS)
            at = wrapped(eighth + off % 8, 8)
            first_turn = (at == 0) | (at == 2) | (at == 5)
            second_turn = (at == 1) | (at == 4) | (at == 6)
            skipped = sum((to >= 4 * n).astype(jnp.int32) for n in (1, 2, 3))

            @pl.when(second_turn if turn else first_turn)
            def _():
                act(pos_copy(j, 2 * to + core))
                act(send_copy(jnp.minimum(to - skipped, HEADS - 1), j, 2 * to + core))

    def start(copy):
        copy.start()

    def left(copy):
        copy.wait_send()

    early = (eighth == 0) | (eighth == 2) | (eighth == 5)
    each_sent(0, start)

    @pl.when(jnp.logical_not(early))
    def _():
        each_sent(0, left)
        each_sent(1, start)

    first = core * BASE

    @pl.when(active)
    def _():
        got[core, SELF] = blocks[my_head]
        pos_in[core, SELF] = pos_out[...]
        held[0:ROWS] = jnp.zeros((ROWS, WIDE), BF16)
        held[ROWS + HELD :] = jnp.zeros((ROWS, WIDE), BF16)
        dkv[...] = jnp.zeros_like(dkv)
        apart = iota((ROWS, 3 * ROWS), 0) - iota((ROWS, 3 * ROWS), 1) + ROWS
        band[...] = jnp.where(jnp.abs(apart) <= ROWS, 0.0, -1e30).astype(F32)
        for pair in range(PAIRS):
            bias[pair] = bias_flat[pair * LANES : (pair + 1) * LANES].reshape(1, LANES)

        def put(n, part, fresh):
            rows = got[part, pl.ds(GROUP * n, GROUP)].reshape(GROUP * ROWS, WIDE)
            there = jnp.concatenate([pos_in[part, GROUP * n + i] for i in range(GROUP)], axis=1) - first
            shape = (TALL, GROUP * ROWS)

            def place(m, _):
                chosen = (jnp.broadcast_to(there - m * TALL, shape) == iota(shape, 0)).astype(F32)
                found = dot(chosen.astype(BF16), rows)
                at = pl.ds(pl.multiple_of(ROWS + m * TALL, ROWS), TALL)
                if not fresh:
                    found = found + held[at].astype(F32)
                held[at] = found.astype(BF16)
                return 0

            lax.fori_loop(0, HELD // TALL, place, 0)

        def take(j, _):
            @pl.when(j != SELF)
            def _():
                pos_copy(j, sibling).wait_recv()
                send_copy(0, j, sibling).wait_recv()

            relay_copy(j, core).start()
            return 0

        def taken(j, _):
            relay_copy(j, 1 - core).wait_recv()
            return 0

        for n in range(CHIPS // GROUP):
            lax.fori_loop(GROUP * n, GROUP * (n + 1), take, 0)
            relay_pos(n, core).start()
            if n == 1:

                @pl.when(early)
                def _():
                    each_sent(1, start)

            put(n, core, n == 0)
            lax.fori_loop(GROUP * n, GROUP * (n + 1), taken, 0)
            relay_pos(n, 1 - core).wait_recv()
            put(n, 1 - core, False)

        places = [pos_in[part, j] for part in range(2) for j in range(CHIPS)]
        places = jnp.concatenate(places + [jnp.zeros((ROWS - PEERS, ROWS), jnp.int32)], axis=0)
        pos_col[...] = jnp.transpose(places.astype(F32)).astype(jnp.int32)

        pair_bias = bias[my_head // 2]
        head_bias = jnp.where(lax.rem(my_head, 2) == 1, swapped(pair_bias), pair_bias)
        head_bias = jnp.where(low[0:1], head_bias, 0.0)
        scale = 1.0 / HEAD_DIM**0.5

        def segment(pos):
            seg = jnp.zeros_like(pos)
            end = jnp.int32(0)
            for utt in range(4):
                end = end + lengths_ref[0, utt]
                seg = seg + (pos >= end).astype(jnp.int32)
            return seg

        def unit(i):
            start = pl.multiple_of((core + i) * ROWS, ROWS)
            at = pl.ds(pl.multiple_of(start + ROWS, ROWS), ROWS)
            window = pl.ds(start, 3 * ROWS)
            here = first + start
            row_pos = here + iota((ROWS, 1), 0)
            col_pos = here - ROWS + iota((1, 3 * ROWS), 1)
            row_seg = segment(row_pos)
            col_seg = jnp.where((col_pos >= 0) & (col_pos < FRAMES), segment(col_pos), -1)
            bg = (held[at, 0:LANES].astype(F32) + head_bias).astype(BF16).astype(F32) * scale
            kv = held[window, LANES:]
            both = jnp.concatenate([jnp.where(low, bg, 0.0), jnp.where(low, 0.0, bg)], axis=0).astype(BF16)
            product = dot_t(both, kv)
            s = jnp.where(row_seg == col_seg, product[:ROWS] + band[...], -1e30)
            top = jnp.max(s, axis=1, keepdims=True)
            e = jnp.exp(s - top)
            p = e * (1.0 / jnp.sum(e, axis=1, keepdims=True))
            prob = p.astype(BF16)
            o = dot(prob, kv).astype(BF16).astype(F32)
            delta = jnp.sum(jnp.where(low, 0.0, bg * o), axis=1, keepdims=True)
            ds = (p * (product[ROWS:] - delta)).astype(BF16)
            dq = dot(ds, kv)
            mine = (i + core >= 2 * core) & (i + core < HALF // ROWS + 2 * core)
            return (
                at,
                window,
                jnp.where(low, dq, o).astype(BF16),
                t_dot(jnp.concatenate([ds, prob], axis=0), both),
                jnp.where(mine, jnp.sum(dq, axis=0, keepdims=True), 0.0),
            )

        def attend(units):
            made = [unit(i) for i in units]
            for at, window, rows, grads, _ in made:
                res[at] = rows
                dkv[window] += grads
            return sum(dq for _, _, _, _, dq in made)

        units = HALF // ROWS // 2
        total = lax.fori_loop(
            0, units, lambda i, total: total + attend((i, i + units)), jnp.zeros((1, LANES), F32)
        )
        gb[...] = total + attend((2 * units,))
        own = pl.ds(pl.multiple_of(ROWS + 2 * ROWS * core, ROWS), HALF)
        results[:, 0:LANES] = res[own]
        results[:, LANES:] = (dkv[own] * (1.0 / scale)).astype(BF16)

    def share_packs(o, _):
        peer = lax.rem(dp + o, PACKS)
        pltpu.make_async_remote_copy(
            src_ref=gb, dst_ref=gb_dp.at[dp],
            send_sem=dp_ss, recv_sem=dp_rs,
            device_id=(peer, me), device_id_type=MESH,
        ).start()
        return 0

    def source(group, at):
        return wrapped(chip - offset(group, at) + CHIPS, CHIPS)

    def make_parts(j):
        own_first = core * HALF
        lane = iota((ROWS, LANES), 1)
        cols = [
            jnp.sum(jnp.where(lane == CHIPS * n + j, pos_col[...], 0), axis=1, keepdims=True) - own_first
            for n in range(2)
        ]
        col = jnp.concatenate(cols, axis=0)
        shape = (2 * ROWS, HALF)
        chosen = (jnp.broadcast_to(col, shape) == iota(shape, 1)).astype(F32).astype(BF16)
        y[...] = dot(chosen, results[...]).astype(BF16)
        part_out[j] = y[pl.ds(pl.multiple_of((1 - core) * ROWS, ROWS), ROWS)]
        ret[j] = y[pl.ds(pl.multiple_of(core * ROWS, ROWS), ROWS)]
        part_copy(j).start()

    def give_back(group, at):
        j = GROUP * group + at
        part_copy(j).wait_recv()
        ret[j] = (ret[j].astype(F32) + part_in[j].astype(F32)).astype(BF16)

        def to_source():
            ret_copy(j, my_head, 2 * source(group, at) + core).start()

        def to_self():
            back[my_head] = ret[j]

        if at == SELF:
            pl.when(group != 0)(to_source)
            pl.when(group == 0)(to_self)
        else:
            to_source()

    def share_head():
        for j in range(CHIPS):
            if j != SELF:
                pltpu.make_async_remote_copy(
                    src_ref=gb_head, dst_ref=gb_heads.at[my_head],
                    send_sem=heads_ss, recv_sem=heads_rs,
                    device_id=(dp, 2 * source(j // GROUP, j % GROUP) + core), device_id_type=MESH,
                ).start()

    @pl.when(active)
    def _():
        def step(group, _):
            make_parts(GROUP * group)

            @pl.when(group >= 1)
            def _():
                give_back(group - 1, GROUP - 1)

            for at in range(1, GROUP):
                make_parts(GROUP * group + at)
                give_back(group, at - 1)

            @pl.when(group == 0)
            def _():
                gb_dp[dp] = gb[...]
                lax.fori_loop(1, PACKS, share_packs, 0)

            @pl.when(group == 1)
            def _():
                many(gb_dp, dp_ss, dp_rs, PACKS - 1).wait_recv()
                gb_half[...] = jnp.sum(gb_dp[...], axis=0)
                half_copy.start()

            @pl.when(group == 2)
            def _():
                half_copy.wait_recv()
                gb_head[...] = gb_half[...] + gb_other[...]
                gb_heads[my_head] = gb_head[...]
                share_head()

            return 0

        lax.fori_loop(0, CHIPS // GROUP, step, 0)
        give_back(CHIPS // GROUP - 1, GROUP - 1)

    outputs = (dq_hbm, o_hbm, dk_hbm, dv_hbm)

    def store(array, pair):
        lanes = slice(pair * LANES, (pair + 1) * LANES)
        return pltpu.make_async_copy(
            x.at[array, :, lanes], outputs[array].at[:, lanes], out_s.at[array, pair]
        )

    for pair in range(PAIRS):
        for head in (2 * pair, 2 * pair + 1):

            @pl.when(chip != chip_of(head))
            def _():
                ret_copy(0, head, sibling).wait_recv()

        lanes = slice(pair * LANES, (pair + 1) * LANES)
        for n in range(2):
            a = back[2 * pair, :, n * LANES : (n + 1) * LANES].astype(F32)
            b = back[2 * pair + 1, :, n * LANES : (n + 1) * LANES].astype(F32)
            x[2 * n, :, lanes] = jnp.where(low, a, swapped(b)).astype(BF16)
            x[2 * n + 1, :, lanes] = jnp.where(low, swapped(a), b).astype(BF16)
        for array in range(4):
            store(array, pair).start()

    @pl.when(active)
    def _():
        many(gb_heads, heads_ss, heads_rs, HEADS - 1).wait_recv()

    @pl.when(jnp.logical_not(active))
    def _():
        many(gb_heads, heads_ss, heads_rs, HEADS).wait_recv()

    for pair in range(PAIRS):
        a, b = gb_heads[2 * pair], gb_heads[2 * pair + 1]
        gb_out[:, pair * LANES : (pair + 1) * LANES] = jnp.where(low[0:1], a, swapped(b))

    @pl.when(active)
    def _():
        many(gb_dp, dp_ss, dp_rs, PACKS - 1).wait_send()
        many(gb_dp, heads_ss, heads_rs, CHIPS - 1).wait_send()
        half_copy.wait_send()
        for n in range(CHIPS // GROUP):
            relay_pos(n, core).wait_send()

    @pl.when(early)
    def _():
        each_sent(0, left)

    each_sent(1, left)

    def given(j, _):
        relay_copy(j, core).wait_send()
        part_copy(j).wait_send()

        @pl.when(j != SELF)
        def _():
            ret_copy(j, my_head, sibling).wait_send()

        return 0

    @pl.when(active)
    def _():
        lax.fori_loop(0, CHIPS, given, 0)

    for pair in range(PAIRS):
        for array in range(4):
            store(array, pair).wait()


def copies(*refs):
    source, target, held = refs[0:5], refs[5:10], refs[10:15]
    flat, in_s, out_s = refs[15:]
    loads = [pltpu.make_async_copy(source[i], held[i], in_s.at[i]) for i in range(5)]
    stores = [pltpu.make_async_copy(held[i], target[i], out_s.at[i]) for i in range(4)]
    stores.append(pltpu.make_async_copy(flat, target[4], out_s.at[4]))
    for load in loads:
        load.start()
    for i in (4, 0, 1, 2, 3):
        loads[i].wait()
        if i == 4:
            flat[...] = held[4][...].reshape(WIDTH)
        stores[i].start()
    for move in stores:
        move.wait()


def body(queries, keys, values, cotangent, pos_bias, owner, slot, lengths):
    vmem = pl.BlockSpec(memory_space=pltpu.VMEM)
    hbm = pl.BlockSpec(memory_space=pltpu.HBM)
    rows = jax.ShapeDtypeStruct((ROWS, WIDTH), BF16)
    row = jax.ShapeDtypeStruct((1, WIDTH), F32)
    dma = pltpu.SemaphoreType.DMA
    i32 = jnp.int32
    results = pl.pallas_call(
        kernel,
        out_shape=(rows, rows, rows, rows, row),
        in_specs=[hbm] * 8,
        out_specs=(hbm,) * 4 + (vmem,),
        scratch_shapes=[
            pltpu.VMEM((4, ROWS, WIDTH), BF16),
            pltpu.VMEM((2 * ROWS, WIDE), BF16),
            pltpu.VMEM((HEADS, ROWS, WIDE), BF16),
            pltpu.VMEM((2, CHIPS, ROWS, WIDE), BF16),
            pltpu.VMEM((1, ROWS), i32),
            pltpu.VMEM((2, CHIPS, 1, ROWS), i32),
            pltpu.VMEM((ROWS, LANES), i32),
            pltpu.VMEM((HELD + 2 * ROWS, WIDE), BF16),
            pltpu.VMEM((ROWS, 3 * ROWS), F32),
            pltpu.VMEM((HELD + 2 * ROWS, LANES), BF16),
            pltpu.VMEM((HELD + 2 * ROWS, LANES), F32),
            pltpu.VMEM((HALF, WIDE), BF16),
            pltpu.VMEM((CHIPS, ROWS, WIDE), BF16),
            pltpu.VMEM((CHIPS, ROWS, WIDE), BF16),
            pltpu.VMEM((CHIPS, ROWS, WIDE), BF16),
            pltpu.VMEM((HEADS, ROWS, WIDE), BF16),
            pltpu.VMEM((WIDTH,), F32),
            pltpu.VMEM((PAIRS, 1, LANES), F32),
            pltpu.VMEM((1, ROWS), i32),
            pltpu.VMEM((1, ROWS), i32),
            pltpu.SMEM((1, 4), i32),
            pltpu.VMEM((1, LANES), F32),
            pltpu.VMEM((PACKS, 1, LANES), F32),
            pltpu.VMEM((1, LANES), F32),
            pltpu.VMEM((1, LANES), F32),
            pltpu.VMEM((1, LANES), F32),
            pltpu.VMEM((HEADS, 1, LANES), F32),
            dma((4,)), dma((4,)), dma((4, PAIRS)),
            dma((CHIPS,)), dma((CHIPS,)), dma((CHIPS,)), dma((CHIPS,)), dma((CHIPS,)), dma((CHIPS,)),
            dma((CHIPS,)), dma((CHIPS,)), dma((CHIPS,)), dma((HEADS,)),
            dma, dma, dma, dma,
            dma((GROUP,)), dma((GROUP,)), dma, dma,
        ],
        compiler_params=pltpu.CompilerParams(
            collective_id=0, has_side_effects=True, vmem_limit_bytes=60 << 20
        ),
    )(
        queries[0], keys[0], values[0], cotangent[0],
        pos_bias, owner, slot, lengths,
    )
    o, dq, dk, dv, gb = pl.pallas_call(
        copies,
        out_shape=(rows, rows, rows, rows, jax.ShapeDtypeStruct((WIDTH,), F32)),
        in_specs=[hbm] * 5,
        out_specs=(hbm,) * 5,
        scratch_shapes=[pltpu.VMEM((ROWS, WIDTH), BF16)] * 4
        + [pltpu.VMEM((1, WIDTH), F32), pltpu.VMEM((WIDTH,), F32), dma((5,)), dma((5,))],
        compiler_params=pltpu.CompilerParams(vmem_limit_bytes=60 << 20),
    )(*results)
    return o[None], dq[None], dk[None], dv[None], gb


def solution(mesh):
    rows = P("dp", "seq", None)
    in_specs = (rows, rows, rows, rows, P(), P("dp", "seq"), P("dp", "seq"), P("dp", None))
    out_specs = (rows, rows, rows, rows, P())
    return jax.shard_map(body, mesh=mesh, in_specs=in_specs, out_specs=out_specs, check_vma=False)
```

```python
import jax
import jax.numpy as jnp
from jax import lax
from jax.experimental import pallas as pl
from jax.experimental.pallas import tpu as pltpu
from jax.sharding import PartitionSpec as P

HEADS = 12
HEAD_DIM = 64
ROWS = 128
WIDTH = HEADS * HEAD_DIM
LANES = 128
WIDE = 256
PAIRS = HEADS // 2
CHIPS = 16
PEERS = 32
PACKS = 16
FRAMES = PEERS * ROWS
HALF = FRAMES // 2
BASE = HALF - 2 * ROWS
HELD = HALF + 2 * ROWS
TALL = 768
GROUP = 4
SELF = 1
MESH = pl.DeviceIdType.MESH
BF16 = jnp.bfloat16
F32 = jnp.float32


def dot(a, b):
    return jnp.dot(a, b, preferred_element_type=F32)


def dot_t(a, b):
    return lax.dot_general(a, b, (((1,), (1,)), ((), ())), preferred_element_type=F32)


def t_dot(a, b):
    return lax.dot_general(a, b, (((0,), (0,)), ((), ())), preferred_element_type=F32)


def iota(shape, dim):
    return lax.broadcasted_iota(jnp.int32, shape, dim)


def wrapped(at, size):
    return jnp.where(at >= size, at - size, at)


def offset(group, at):
    return (8, CHIPS, 1, 9)[at] + (-1, -1, 1, 1)[at] * group


def chip_of(head):
    return head // 3 * 4 + head % 3


def kernel(
    q_hbm, k_hbm, v_hbm, g_hbm, bias_hbm, owner_hbm, slot_hbm, lengths_hbm,
    o_hbm, dq_hbm, dk_hbm, dv_hbm, gb_out,
    x, y, blocks, got, pos_out, pos_in, pos_col,
    held, band, res, dkv, results, part_out, part_in, ret, back,
    bias_flat, bias, owner_ref, slot_ref, lengths_ref,
    gb, gb_dp, gb_half, gb_other, gb_head, gb_heads,
    small_s, in_s, out_s,
    blocks_ss, got_rs, pos_ss, pos_rs, relay_ss, relay_rs,
    part_ss, part_rs, ret_ss, back_rs, heads_ss, heads_rs, dp_ss, dp_rs,
    relay_pos_ss, relay_pos_rs, half_ss, half_rs,
):
    dp = lax.axis_index("dp")
    me = lax.axis_index("seq")
    chip = me // 2
    core = lax.rem(me, 2)
    sibling = me + 1 - 2 * core
    active = lax.rem(chip, 4) < 3
    my_head = jnp.minimum(chip // 4 * 3 + lax.rem(chip, 4), HEADS - 1)

    barrier = pltpu.get_barrier_semaphore()

    def greet_seq(o, _):
        peer = lax.rem(me + o, PEERS)
        pl.semaphore_signal(barrier, inc=1, device_id=(dp, peer), device_id_type=MESH)
        return 0

    def greet_dp(o, _):
        peer = lax.rem(dp + o, PACKS)
        pl.semaphore_signal(barrier, inc=1, device_id=(peer, me), device_id_type=MESH)
        return 0

    lax.fori_loop(1, PEERS, greet_seq, 0)
    lax.fori_loop(1, PACKS, greet_dp, 0)

    inputs = (q_hbm, g_hbm, k_hbm, v_hbm)
    loads = [pltpu.make_async_copy(inputs[i], x.at[i], in_s.at[i]) for i in range(4)]
    small = [
        pltpu.make_async_copy(src, dst, small_s.at[i])
        for i, (src, dst) in enumerate(
            [
                (owner_hbm, owner_ref),
                (slot_hbm, slot_ref),
                (bias_hbm, bias_flat),
                (lengths_hbm, lengths_ref),
            ]
        )
    ]
    for copy in small + loads:
        copy.start()
    for copy in small:
        copy.wait()
    pos_out[...] = owner_ref[...] * ROWS + slot_ref[...]

    low = iota((ROWS, LANES), 1) < HEAD_DIM

    def swapped(a):
        return pltpu.roll(a, HEAD_DIM, 1)

    for copy in loads:
        copy.wait()
    for pair in range(PAIRS):
        lanes = slice(pair * LANES, (pair + 1) * LANES)
        q, g, k, v = (x[i, :, lanes].astype(F32) for i in range(4))
        for at, (a, b) in ((0, (q, g)), (LANES, (k, v))):
            blocks[2 * pair, :, at : at + LANES] = jnp.where(low, a, swapped(b)).astype(BF16)
            blocks[2 * pair + 1, :, at : at + LANES] = jnp.where(low, swapped(a), b).astype(BF16)

    def send_copy(head, j, peer):
        return pltpu.make_async_remote_copy(
            src_ref=blocks.at[head], dst_ref=got.at[core, j],
            send_sem=blocks_ss.at[j], recv_sem=got_rs.at[j],
            device_id=(dp, peer), device_id_type=MESH,
        )

    def relay_copy(j, part):
        return pltpu.make_async_remote_copy(
            src_ref=got.at[part, j], dst_ref=got.at[part, j],
            send_sem=relay_ss.at[j], recv_sem=relay_rs.at[j],
            device_id=(dp, sibling), device_id_type=MESH,
        )

    def part_copy(j):
        return pltpu.make_async_remote_copy(
            src_ref=part_out.at[j], dst_ref=part_in.at[j],
            send_sem=part_ss.at[j], recv_sem=part_rs.at[j],
            device_id=(dp, sibling), device_id_type=MESH,
        )

    def ret_copy(j, head, peer):
        return pltpu.make_async_remote_copy(
            src_ref=ret.at[j], dst_ref=back.at[head],
            send_sem=ret_ss.at[j], recv_sem=back_rs.at[head],
            device_id=(dp, peer), device_id_type=MESH,
        )

    def many(buf, send_sem, recv_sem, count):
        return pltpu.make_async_remote_copy(
            src_ref=buf.at[pl.ds(0, count)], dst_ref=buf.at[pl.ds(0, count)],
            send_sem=send_sem, recv_sem=recv_sem,
            device_id=(dp, sibling), device_id_type=MESH,
        )

    pl.semaphore_wait(barrier, PEERS - 1 + PACKS - 1)

    def pos_copy(j, peer):
        return pltpu.make_async_remote_copy(
            src_ref=pos_out, dst_ref=pos_in.at[core, j],
            send_sem=pos_ss.at[j], recv_sem=pos_rs.at[j],
            device_id=(dp, peer), device_id_type=MESH,
        )

    def relay_pos(n, part):
        rows = pl.ds(GROUP * n, GROUP)
        return pltpu.make_async_remote_copy(
            src_ref=pos_in.at[part, rows], dst_ref=pos_in.at[part, rows],
            send_sem=relay_pos_ss.at[n], recv_sem=relay_pos_rs.at[n],
            device_id=(dp, sibling), device_id_type=MESH,
        )

    half_copy = pltpu.make_async_remote_copy(
        src_ref=gb_half, dst_ref=gb_other,
        send_sem=half_ss, recv_sem=half_rs,
        device_id=(dp, sibling), device_id_type=MESH,
    )

    eighth = lax.rem(chip, 8)

    def each_sent(turn, act, begin=0, end=CHIPS):
        for j in range(begin, end):
            if j == SELF:
                continue
            off = offset(j // GROUP, j % GROUP) % CHIPS
            to = wrapped(chip + off, CHIPS)
            at = wrapped(eighth + off % 8, 8)
            first_turn = (at == 0) | (at == 2) | (at == 5)
            second_turn = (at == 1) | (at == 4) | (at == 6)
            skipped = sum((to >= 4 * n).astype(jnp.int32) for n in (1, 2, 3))

            @pl.when(second_turn if turn else first_turn)
            def _():
                act(pos_copy(j, 2 * to + core))
                act(send_copy(jnp.minimum(to - skipped, HEADS - 1), j, 2 * to + core))

    def start(copy):
        copy.start()

    def left(copy):
        copy.wait_send()

    early = (eighth == 0) | (eighth == 2) | (eighth == 5)
    each_sent(0, start)

    @pl.when(jnp.logical_not(early))
    def _():
        each_sent(0, left)
        each_sent(1, start)

    first = core * BASE

    @pl.when(active)
    def _():
        got[core, SELF] = blocks[my_head]
        pos_in[core, SELF] = pos_out[...]
        held[0:ROWS] = jnp.zeros((ROWS, WIDE), BF16)
        held[ROWS + HELD :] = jnp.zeros((ROWS, WIDE), BF16)
        dkv[...] = jnp.zeros_like(dkv)
        apart = iota((ROWS, 3 * ROWS), 0) - iota((ROWS, 3 * ROWS), 1) + ROWS
        band[...] = jnp.where(jnp.abs(apart) <= ROWS, 0.0, -1e30).astype(F32)
        for pair in range(PAIRS):
            bias[pair] = bias_flat[pair * LANES : (pair + 1) * LANES].reshape(1, LANES)

        def put(n, part, fresh):
            rows = got[part, pl.ds(GROUP * n, GROUP)].reshape(GROUP * ROWS, WIDE)
            there = jnp.concatenate([pos_in[part, GROUP * n + i] for i in range(GROUP)], axis=1) - first
            shape = (TALL, GROUP * ROWS)

            def place(m, _):
                chosen = (jnp.broadcast_to(there - m * TALL, shape) == iota(shape, 0)).astype(F32)
                found = dot(chosen.astype(BF16), rows)
                at = pl.ds(pl.multiple_of(ROWS + m * TALL, ROWS), TALL)
                if not fresh:
                    found = found + held[at].astype(F32)
                held[at] = found.astype(BF16)
                return 0

            lax.fori_loop(0, HELD // TALL, place, 0)

        def take(j, _):
            @pl.when(j != SELF)
            def _():
                pos_copy(j, sibling).wait_recv()
                send_copy(0, j, sibling).wait_recv()

            relay_copy(j, core).start()
            return 0

        def taken(j, _):
            relay_copy(j, 1 - core).wait_recv()
            return 0

        for n in range(CHIPS // GROUP):
            lax.fori_loop(GROUP * n, GROUP * (n + 1), take, 0)
            relay_pos(n, core).start()
            if n == 1:

                @pl.when(early)
                def _():
                    each_sent(1, start)

            put(n, core, n == 0)
            lax.fori_loop(GROUP * n, GROUP * (n + 1), taken, 0)
            relay_pos(n, 1 - core).wait_recv()
            put(n, 1 - core, False)

        places = [pos_in[part, j] for part in range(2) for j in range(CHIPS)]
        places = jnp.concatenate(places + [jnp.zeros((ROWS - PEERS, ROWS), jnp.int32)], axis=0)
        pos_col[...] = jnp.transpose(places.astype(F32)).astype(jnp.int32)

        pair_bias = bias[my_head // 2]
        head_bias = jnp.where(lax.rem(my_head, 2) == 1, swapped(pair_bias), pair_bias)
        head_bias = jnp.where(low[0:1], head_bias, 0.0)
        scale = 1.0 / HEAD_DIM**0.5

        def segment(pos):
            seg = jnp.zeros_like(pos)
            end = jnp.int32(0)
            for utt in range(4):
                end = end + lengths_ref[0, utt]
                seg = seg + (pos >= end).astype(jnp.int32)
            return seg

        def unit(i):
            start = pl.multiple_of((core + i) * ROWS, ROWS)
            at = pl.ds(pl.multiple_of(start + ROWS, ROWS), ROWS)
            window = pl.ds(start, 3 * ROWS)
            here = first + start
            row_pos = here + iota((ROWS, 1), 0)
            col_pos = here - ROWS + iota((1, 3 * ROWS), 1)
            row_seg = segment(row_pos)
            col_seg = jnp.where((col_pos >= 0) & (col_pos < FRAMES), segment(col_pos), -1)
            bg = (held[at, 0:LANES].astype(F32) + head_bias).astype(BF16).astype(F32) * scale
            kv = held[window, LANES:]
            both = jnp.concatenate([jnp.where(low, bg, 0.0), jnp.where(low, 0.0, bg)], axis=0).astype(BF16)
            product = dot_t(both, kv)
            s = jnp.where(row_seg == col_seg, product[:ROWS] + band[...], -1e30)
            top = jnp.max(s, axis=1, keepdims=True)
            e = jnp.exp(s - top)
            p = e * (1.0 / jnp.sum(e, axis=1, keepdims=True))
            prob = p.astype(BF16)
            o = dot(prob, kv).astype(BF16).astype(F32)
            delta = jnp.sum(jnp.where(low, 0.0, bg * o), axis=1, keepdims=True)
            ds = (p * (product[ROWS:] - delta)).astype(BF16)
            dq = dot(ds, kv)
            mine = (i + core >= 2 * core) & (i + core < HALF // ROWS + 2 * core)
            return (
                at,
                window,
                jnp.where(low, dq, o).astype(BF16),
                t_dot(jnp.concatenate([ds, prob], axis=0), both),
                jnp.where(mine, jnp.sum(dq, axis=0, keepdims=True), 0.0),
            )

        def attend(units):
            made = [unit(i) for i in units]
            for at, window, rows, grads, _ in made:
                res[at] = rows
                dkv[window] += grads
            return sum(dq for _, _, _, _, dq in made)

        units = HALF // ROWS // 2
        total = lax.fori_loop(
            0, units, lambda i, total: total + attend((i, i + units)), jnp.zeros((1, LANES), F32)
        )
        gb[...] = total + attend((2 * units,))
        own = pl.ds(pl.multiple_of(ROWS + 2 * ROWS * core, ROWS), HALF)
        results[:, 0:LANES] = res[own]
        results[:, LANES:] = (dkv[own] * (1.0 / scale)).astype(BF16)

    def share_packs(o, _):
        peer = lax.rem(dp + o, PACKS)
        pltpu.make_async_remote_copy(
            src_ref=gb, dst_ref=gb_dp.at[dp],
            send_sem=dp_ss, recv_sem=dp_rs,
            device_id=(peer, me), device_id_type=MESH,
        ).start()
        return 0

    def source(group, at):
        return wrapped(chip - offset(group, at) + CHIPS, CHIPS)

    def make_parts(j):
        own_first = core * HALF
        lane = iota((ROWS, LANES), 1)
        cols = [
            jnp.sum(jnp.where(lane == CHIPS * n + j, pos_col[...], 0), axis=1, keepdims=True) - own_first
            for n in range(2)
        ]
        col = jnp.concatenate(cols, axis=0)
        shape = (2 * ROWS, HALF)
        chosen = (jnp.broadcast_to(col, shape) == iota(shape, 1)).astype(F32).astype(BF16)
        y[...] = dot(chosen, results[...]).astype(BF16)
        part_out[j] = y[pl.ds(pl.multiple_of((1 - core) * ROWS, ROWS), ROWS)]
        ret[j] = y[pl.ds(pl.multiple_of(core * ROWS, ROWS), ROWS)]
        part_copy(j).start()

    def give_back(group, at):
        j = GROUP * group + at
        part_copy(j).wait_recv()
        ret[j] = (ret[j].astype(F32) + part_in[j].astype(F32)).astype(BF16)

        def to_source():
            ret_copy(j, my_head, 2 * source(group, at) + core).start()

        def to_self():
            back[my_head] = ret[j]

        if at == SELF:
            pl.when(group != 0)(to_source)
            pl.when(group == 0)(to_self)
        else:
            to_source()

    def share_head():
        for j in range(CHIPS):
            if j != SELF:
                pltpu.make_async_remote_copy(
                    src_ref=gb_head, dst_ref=gb_heads.at[my_head],
                    send_sem=heads_ss, recv_sem=heads_rs,
                    device_id=(dp, 2 * source(j // GROUP, j % GROUP) + core), device_id_type=MESH,
                ).start()

    @pl.when(active)
    def _():
        def step(group, _):
            make_parts(GROUP * group)

            @pl.when(group >= 1)
            def _():
                give_back(group - 1, GROUP - 1)

            for at in range(1, GROUP):
                make_parts(GROUP * group + at)
                give_back(group, at - 1)

            @pl.when(group == 0)
            def _():
                gb_dp[dp] = gb[...]
                lax.fori_loop(1, PACKS, share_packs, 0)

            @pl.when(group == 2)
            def _():
                many(gb_dp, dp_ss, dp_rs, PACKS - 1).wait_recv()
                gb_half[...] = jnp.sum(gb_dp[...], axis=0)
                half_copy.start()

            @pl.when(group == 3)
            def _():
                half_copy.wait_recv()
                gb_head[...] = gb_half[...] + gb_other[...]
                gb_heads[my_head] = gb_head[...]
                share_head()

            return 0

        lax.fori_loop(0, CHIPS // GROUP, step, 0)
        give_back(CHIPS // GROUP - 1, GROUP - 1)

    outputs = (dq_hbm, o_hbm, dk_hbm, dv_hbm)

    def store(array, pair):
        lanes = slice(pair * LANES, (pair + 1) * LANES)
        return pltpu.make_async_copy(
            x.at[array, :, lanes], outputs[array].at[:, lanes], out_s.at[array, pair]
        )

    for pair in range(PAIRS):
        for head in (2 * pair, 2 * pair + 1):

            @pl.when(chip != chip_of(head))
            def _():
                ret_copy(0, head, sibling).wait_recv()

        lanes = slice(pair * LANES, (pair + 1) * LANES)
        for n in range(2):
            a = back[2 * pair, :, n * LANES : (n + 1) * LANES].astype(F32)
            b = back[2 * pair + 1, :, n * LANES : (n + 1) * LANES].astype(F32)
            x[2 * n, :, lanes] = jnp.where(low, a, swapped(b)).astype(BF16)
            x[2 * n + 1, :, lanes] = jnp.where(low, swapped(a), b).astype(BF16)
        for array in range(4):
            store(array, pair).start()

    @pl.when(active)
    def _():
        many(gb_heads, heads_ss, heads_rs, HEADS - 1).wait_recv()

    @pl.when(jnp.logical_not(active))
    def _():
        many(gb_heads, heads_ss, heads_rs, HEADS).wait_recv()

    for pair in range(PAIRS):
        a, b = gb_heads[2 * pair], gb_heads[2 * pair + 1]
        gb_out[:, pair * LANES : (pair + 1) * LANES] = jnp.where(low[0:1], a, swapped(b))

    @pl.when(active)
    def _():
        many(gb_dp, dp_ss, dp_rs, PACKS - 1).wait_send()
        many(gb_dp, heads_ss, heads_rs, CHIPS - 1).wait_send()
        half_copy.wait_send()
        for n in range(CHIPS // GROUP):
            relay_pos(n, core).wait_send()

    @pl.when(early)
    def _():
        each_sent(0, left)

    each_sent(1, left)

    def given(j, _):
        relay_copy(j, core).wait_send()
        part_copy(j).wait_send()

        @pl.when(j != SELF)
        def _():
            ret_copy(j, my_head, sibling).wait_send()

        return 0

    @pl.when(active)
    def _():
        lax.fori_loop(0, CHIPS, given, 0)

    for pair in range(PAIRS):
        for array in range(4):
            store(array, pair).wait()


def copies(*refs):
    source, target, held = refs[0:5], refs[5:10], refs[10:15]
    flat, in_s, out_s = refs[15:]
    loads = [pltpu.make_async_copy(source[i], held[i], in_s.at[i]) for i in range(5)]
    stores = [pltpu.make_async_copy(held[i], target[i], out_s.at[i]) for i in range(4)]
    stores.append(pltpu.make_async_copy(flat, target[4], out_s.at[4]))
    for load in loads:
        load.start()
    for i in (4, 0, 1, 2, 3):
        loads[i].wait()
        if i == 4:
            flat[...] = held[4][...].reshape(WIDTH)
        stores[i].start()
    for move in stores:
        move.wait()


def body(queries, keys, values, cotangent, pos_bias, owner, slot, lengths):
    vmem = pl.BlockSpec(memory_space=pltpu.VMEM)
    hbm = pl.BlockSpec(memory_space=pltpu.HBM)
    rows = jax.ShapeDtypeStruct((ROWS, WIDTH), BF16)
    row = jax.ShapeDtypeStruct((1, WIDTH), F32)
    dma = pltpu.SemaphoreType.DMA
    i32 = jnp.int32
    results = pl.pallas_call(
        kernel,
        out_shape=(rows, rows, rows, rows, row),
        in_specs=[hbm] * 8,
        out_specs=(hbm,) * 4 + (vmem,),
        scratch_shapes=[
            pltpu.VMEM((4, ROWS, WIDTH), BF16),
            pltpu.VMEM((2 * ROWS, WIDE), BF16),
            pltpu.VMEM((HEADS, ROWS, WIDE), BF16),
            pltpu.VMEM((2, CHIPS, ROWS, WIDE), BF16),
            pltpu.VMEM((1, ROWS), i32),
            pltpu.VMEM((2, CHIPS, 1, ROWS), i32),
            pltpu.VMEM((ROWS, LANES), i32),
            pltpu.VMEM((HELD + 2 * ROWS, WIDE), BF16),
            pltpu.VMEM((ROWS, 3 * ROWS), F32),
            pltpu.VMEM((HELD + 2 * ROWS, LANES), BF16),
            pltpu.VMEM((HELD + 2 * ROWS, LANES), F32),
            pltpu.VMEM((HALF, WIDE), BF16),
            pltpu.VMEM((CHIPS, ROWS, WIDE), BF16),
            pltpu.VMEM((CHIPS, ROWS, WIDE), BF16),
            pltpu.VMEM((CHIPS, ROWS, WIDE), BF16),
            pltpu.VMEM((HEADS, ROWS, WIDE), BF16),
            pltpu.VMEM((WIDTH,), F32),
            pltpu.VMEM((PAIRS, 1, LANES), F32),
            pltpu.VMEM((1, ROWS), i32),
            pltpu.VMEM((1, ROWS), i32),
            pltpu.SMEM((1, 4), i32),
            pltpu.VMEM((1, LANES), F32),
            pltpu.VMEM((PACKS, 1, LANES), F32),
            pltpu.VMEM((1, LANES), F32),
            pltpu.VMEM((1, LANES), F32),
            pltpu.VMEM((1, LANES), F32),
            pltpu.VMEM((HEADS, 1, LANES), F32),
            dma((4,)), dma((4,)), dma((4, PAIRS)),
            dma((CHIPS,)), dma((CHIPS,)), dma((CHIPS,)), dma((CHIPS,)), dma((CHIPS,)), dma((CHIPS,)),
            dma((CHIPS,)), dma((CHIPS,)), dma((CHIPS,)), dma((HEADS,)),
            dma, dma, dma, dma,
            dma((GROUP,)), dma((GROUP,)), dma, dma,
        ],
        compiler_params=pltpu.CompilerParams(
            collective_id=0, has_side_effects=True, vmem_limit_bytes=60 << 20
        ),
    )(
        queries[0], keys[0], values[0], cotangent[0],
        pos_bias, owner, slot, lengths,
    )
    o, dq, dk, dv, gb = pl.pallas_call(
        copies,
        out_shape=(rows, rows, rows, rows, jax.ShapeDtypeStruct((WIDTH,), F32)),
        in_specs=[hbm] * 5,
        out_specs=(hbm,) * 5,
        scratch_shapes=[pltpu.VMEM((ROWS, WIDTH), BF16)] * 4
        + [pltpu.VMEM((1, WIDTH), F32), pltpu.VMEM((WIDTH,), F32), dma((5,)), dma((5,))],
        compiler_params=pltpu.CompilerParams(vmem_limit_bytes=60 << 20),
    )(*results)
    return o[None], dq[None], dk[None], dv[None], gb


def solution(mesh):
    rows = P("dp", "seq", None)
    in_specs = (rows, rows, rows, rows, P(), P("dp", "seq"), P("dp", "seq"), P("dp", None))
    out_specs = (rows, rows, rows, rows, P())
    return jax.shard_map(body, mesh=mesh, in_specs=in_specs, out_specs=out_specs, check_vma=False)
```
